128 devices in a mesh: grp: 16 (over z, x), tp: 8 (over y, core).
Axes of the slice: x: 4, y: 4, z: 4, core: 2. Of those that a mesh axis runs over, the one named last changes fastest.
Arguments:
- hidden: bfloat16 [8192, 12288], P('grp', 'tp'), may hold values from -6 to 6
- queries: bfloat16 [8192, 12288], P('grp', 'tp'), may hold values from -25 to 25
- keyval_weight: bfloat16 [12288, 2, 1024], P(None, None, 'tp'), may hold values from -0.0546875 to 0.0546875
- keyval_pool: bfloat16 [1280, 2, 8, 128, 128], P('grp', None, 'tp'), may hold values from -6 to 6
- prefix_len: int32 [32], replicated, may hold values from 128 to 4096, as said below
- slot_request: int32 [32], replicated, may hold values from 0 to 31, as said below
- hit_holder: int32 [32, 32], replicated, may hold values from 0 to 15, as said below
- hit_slot: int32 [32, 32], replicated, may hold values from 0 to 79, as said below
- new_owner: int32 [32, 2], replicated, may hold values from 0 to 15, as said below
- new_slot: int32 [32, 2], replicated, may hold values from 0 to 79, as said below
Outputs:
- attention: bfloat16 [8192, 12288], P('grp', 'tp')
- new_pool: bfloat16 [1280, 2, 8, 128, 128], P('grp', None, 'tp')
The draws below stay inside these ranges and needn't reach their ends.
Inputs may be any that keep to these rules, and one draw needn't show every extreme that they name: `prefix_len`: every request of some group (slots g * 2 to g * 2 + 1) has exactly 4096. `slot_request`: a permutation; group g serves the requests in slots g * 2 to g * 2 + 1, and its rows of hidden and queries stand in that order. `hit_holder`: block b of request r is live iff b * 128 < prefix_len[r]; other entries are to be ignored. Among all 64 entries of one group's requests, live or not, no holder is named more than 4 times, and in the group whose prefixes are full some holder is named exactly 4 times. `hit_slot`: all entries name different pool rows, none of them a row that new_owner and new_slot name. `new_owner`: the 4 new blocks of one group's requests have different owners. `new_slot`: all new blocks name different pool rows.
All inputs are finite; a program needn't handle non-finite values.
Results may differ from the reference program's by a relative error of at most 0.025.
Values may be sent and summed in bfloat16 or wider, within the bound.
A program may use at most 128 MiB of HBM per device.

```python
import math
import jax
import jax.numpy as jnp
from jax import lax

D = 12288
HQ = 96
KVH = 8
HD = 128
BLK = 128
STRETCH = 256
REQ_GRP = 2
MAXB = 32
NEWB = 2
REQ = 32
TOKENS = 8192
CAP = 4
POOL_DEV = 80
POOL = 1280


def plan_tables(key):
    groups = REQ // REQ_GRP
    item_count = REQ_GRP * MAXB
    fresh_count = REQ_GRP * NEWB
    key_map, key_len, key_full, key_hold, key_slot, key_own = jax.random.split(key, 6)
    slot_request = jax.random.permutation(key_map, REQ).astype(jnp.int32)
    reach = MAXB * BLK - BLK
    spread = jax.random.randint(key_len, (REQ,), 0, reach + 1)
    lengths = BLK + spread * spread // max(reach, 1)
    full_group = jax.random.randint(key_full, (), 0, groups)
    slot_group = jnp.arange(REQ, dtype=jnp.int32) // REQ_GRP
    lengths = jnp.where(slot_group == full_group, MAXB * BLK, lengths).astype(jnp.int32)

    def shuffle_items(subkey):
        return jax.random.permutation(subkey, item_count)

    def shuffle_slots(subkey):
        return jax.random.permutation(subkey, POOL_DEV)

    def shuffle_groups(subkey):
        return jax.random.permutation(subkey, groups)
    orders = jax.vmap(shuffle_items)(jax.random.split(key_hold, groups)).astype(jnp.int32)
    group_ids = jnp.arange(groups, dtype=jnp.int32)[:, None]
    stride = groups // 2 + 1
    holders = (group_ids - 1 + groups + orders * stride) % groups
    rank_of = orders // groups
    slot_perm = jax.vmap(shuffle_slots)(jax.random.split(key_slot, groups)).astype(jnp.int32)
    hit_slots = slot_perm[holders, group_ids * CAP + rank_of]
    owner_perm = jax.vmap(shuffle_groups)(jax.random.split(key_own, groups)).astype(jnp.int32)
    owners = owner_perm[:, :fresh_count]
    owner_slots = slot_perm[owners, groups * CAP + group_ids]

    def by_request(values):
        return jnp.zeros_like(values).at[slot_request].set(values)
    return (slot_request, by_request(lengths), by_request(holders.reshape(REQ, MAXB)), by_request(hit_slots.reshape(REQ, MAXB)), by_request(owners.reshape(REQ, NEWB)), by_request(owner_slots.reshape(REQ, NEWB)))


def draw_slot_request(key, part):
    return plan_tables(key)[0]


def draw_prefix_len(key, part):
    return plan_tables(key)[1]


def draw_hit_holder(key, part):
    return plan_tables(key)[2]


def draw_hit_slot(key, part):
    return plan_tables(key)[3]


def draw_new_owner(key, part):
    return plan_tables(key)[4]


def draw_new_slot(key, part):
    return plan_tables(key)[5]


def draw_queries(key, part):
    key = jax.random.fold_in(key, 11)
    result = jnp.clip(jax.random.normal(key, (TOKENS, HQ, HD), jnp.float32), -6.0, 6.0)
    return result.reshape(TOKENS, HQ * HD).astype(jnp.bfloat16)


def draw_keyval_pool(key, part):
    key = jax.random.fold_in(key, 12)
    shape = (POOL, 2, KVH, BLK, HD)
    result = jnp.clip(jax.random.normal(key, shape, jnp.float32), -6.0, 6.0)
    return result.astype(jnp.bfloat16)


def block_scale(rng, extent, shards, smallest, largest):
    loudness, own = 1.0, jax.random.fold_in(rng, 6)
    for position, shards_of in shards:
        draws = jnp.exp(jax.random.uniform(jax.random.fold_in(own, position), (shards_of,), jnp.float32, smallest / len(shards), largest / len(shards)))
        loudness = loudness * jnp.repeat(draws, extent[position] // shards_of).reshape([-1 if axis == position else 1 for axis in range(len(extent))])
    return loudness


def noise(own_key, shape, width, bound, cuts=(), held_as=jnp.bfloat16):
    gain = block_scale(own_key, shape, cuts, -0.22, 0.18) if cuts else 1.0
    values = jax.random.normal(own_key, shape, jnp.float32) * width * gain
    return jnp.minimum(jnp.maximum(values, -bound), bound).astype(held_as)


def setup_inputs(seed: int = 0) -> dict:
    splits = jax.random.split(jax.random.key(seed), 11)
    hidden = noise(splits[0], (TOKENS, D), 1.0, 6.0, ((0, 16), (1, 8)))
    queries = draw_queries(jax.random.fold_in(splits[10], 71), 0)
    keyval_weight = noise(splits[2], (D, 2, KVH * HD), D ** -0.5, 0.0546875, ((2, 8),))
    keyval_pool = draw_keyval_pool(jax.random.fold_in(splits[10], 71), 0)
    prefix_len = draw_prefix_len(jax.random.fold_in(splits[10], 71), 0)
    slot_request = draw_slot_request(jax.random.fold_in(splits[10], 71), 0)
    hit_holder = draw_hit_holder(jax.random.fold_in(splits[10], 71), 0)
    hit_slot = draw_hit_slot(jax.random.fold_in(splits[10], 71), 0)
    new_owner = draw_new_owner(jax.random.fold_in(splits[10], 71), 0)
    new_slot = draw_new_slot(jax.random.fold_in(splits[10], 71), 0)
    return dict(hidden=hidden, queries=queries, keyval_weight=keyval_weight, keyval_pool=keyval_pool, prefix_len=prefix_len, slot_request=slot_request, hit_holder=hit_holder, hit_slot=hit_slot, new_owner=new_owner, new_slot=new_slot)


ROPE_BASE = 1000000.0
MASKED_SCORE = -1e+30

def rotate(key_block, positions):
    half_dim = key_block.shape[-1] // 2
    frequency = ROPE_BASE ** (-(jnp.arange(half_dim, dtype=jnp.float32) * 2.0 / key_block.shape[-1]))
    angles = positions.astype(jnp.float32)[:, None] * frequency[None, :]
    cosine = jnp.cos(angles)
    sine_part = jnp.sin(angles)
    front_half = key_block[..., :half_dim]
    back_half = key_block[..., half_dim:]
    return jnp.concatenate([front_half * cosine - back_half * sine_part, back_half * cosine + front_half * sine_part], axis=-1)

def reference(hidden, queries, keyval_weight, keyval_pool, prefix_len, slot_request, hit_holder, hit_slot, new_owner, new_slot):
    grouping = HQ // KVH
    score_scale = 1.0 / math.sqrt(HD)
    projected = jnp.dot(hidden, keyval_weight.reshape(D, 2 * KVH * HD), preferred_element_type=jnp.float32)
    projected = projected.reshape(REQ, STRETCH, 2, KVH, HD)
    lengths = prefix_len[slot_request]
    positions = lengths[:, None] + jnp.arange(STRETCH, dtype=jnp.int32)[None, :]
    keys_new = jax.vmap(rotate)(jnp.transpose(projected[:, :, 0], (0, 2, 1, 3)), positions).astype(jnp.bfloat16)
    values_new = jnp.transpose(projected[:, :, 1], (0, 2, 1, 3)).astype(jnp.bfloat16)
    stacked = jnp.stack([keys_new, values_new], axis=1).reshape(REQ, 2, KVH, NEWB, BLK, HD)
    stacked = jnp.transpose(stacked, (0, 3, 1, 2, 4, 5)).reshape(REQ * NEWB, 2, KVH, BLK, HD)
    indices = (new_owner[slot_request] * POOL_DEV + new_slot[slot_request]).reshape(REQ * NEWB)
    new_pool = keyval_pool.at[indices].set(stacked)
    query_rows = queries.reshape(REQ, STRETCH, KVH, grouping, HD)
    key_count = MAXB * BLK + STRETCH
    key_pos = jnp.arange(key_count, dtype=jnp.int32)
    token_pos = jnp.arange(STRETCH, dtype=jnp.int32)

    def attend_slot(slot):
        request = slot_request[slot]
        length = prefix_len[request]
        pool_rows = hit_holder[request] * POOL_DEV + hit_slot[request]
        blocks = keyval_pool[pool_rows]
        old_keys = jnp.transpose(blocks[:, 0], (1, 0, 2, 3)).reshape(KVH, MAXB * BLK, HD)
        old_values = jnp.transpose(blocks[:, 1], (1, 0, 2, 3)).reshape(KVH, MAXB * BLK, HD)
        all_keys = jnp.concatenate([old_keys, keys_new[slot]], axis=1).astype(jnp.float32)
        all_values = jnp.concatenate([old_values, values_new[slot]], axis=1).astype(jnp.float32)
        query = query_rows[slot].astype(jnp.float32)
        scores = jnp.einsum('tjgd,jkd->jtgk', query, all_keys) * score_scale
        from_prefix = (key_pos[None, :] < MAXB * BLK) & (key_pos[None, :] < length)
        from_stretch = (key_pos[None, :] >= MAXB * BLK) & (key_pos[None, :] - MAXB * BLK <= token_pos[:, None])
        visible = (from_prefix | from_stretch)[None, :, None, :]
        scores = jnp.where(visible, scores, MASKED_SCORE)
        row_max = lax.optimization_barrier(jnp.max(scores, axis=-1, keepdims=True))
        weights = jnp.where(visible, jnp.exp(scores - row_max), 0.0)
        weight_sum = lax.optimization_barrier(jnp.sum(weights, axis=-1))
        rounded = lax.optimization_barrier(weights.astype(jnp.bfloat16)).astype(jnp.float32)
        combined = jnp.einsum('jtgk,jkd->tjgd', rounded, all_values)
        combined = combined / jnp.transpose(weight_sum, (1, 0, 2))[..., None]
        return combined.astype(jnp.bfloat16).reshape(STRETCH, HQ * HD)
    attention = lax.map(attend_slot, jnp.arange(REQ, dtype=jnp.int32)).reshape(TOKENS, HQ * HD)
    return (attention, new_pool)
```

```python
import functools
import math

import jax
import jax.numpy as jnp
from jax import lax
from jax.experimental import pallas as pl
from jax.experimental.pallas import tpu as pltpu
from jax.sharding import PartitionSpec as P

MESH = pl.DeviceIdType.MESH
ROPE_BASE = 1000000.0
MASKED = -1e30
BLK = 128
HD = 128
ROUNDS = 4
PER_ROUND = 8
HEADS_PER_STEP = 6
bf16 = jnp.bfloat16
f32 = jnp.float32


def remote(src, dst, send_sem, recv_sem, device):
    return pltpu.make_async_remote_copy(
        src_ref=src,
        dst_ref=dst,
        send_sem=send_sem,
        recv_sem=recv_sem,
        device_id=device,
        device_id_type=MESH,
    )


def drain(ref, sem):
    pltpu.make_async_copy(ref, ref, sem).wait()


def gather_kernel(rows_ref, pool_ref, out_ref, sem):
    count = out_ref.shape[0]

    def go(i, _):
        pltpu.make_async_copy(pool_ref.at[rows_ref[i]], out_ref.at[i], sem).start()
        return 0

    lax.fori_loop(0, count, go, 0)
    drain(out_ref, sem)


def patch_kernel(rows_ref, pool_ref, pushed_ref, out_ref, sem):
    del pool_ref
    count = pushed_ref.shape[0]
    limit = out_ref.shape[0]

    def go(i, _):
        @pl.when(rows_ref[i] < limit)
        def _():
            pltpu.make_async_copy(pushed_ref.at[i], out_ref.at[rows_ref[i]], sem.at[i]).start()

        return 0

    def done(i, _):
        @pl.when(rows_ref[i] < limit)
        def _():
            pltpu.make_async_copy(pushed_ref.at[i], out_ref.at[rows_ref[i]], sem.at[i]).wait()

        return 0

    lax.fori_loop(0, count, go, 0)
    lax.fori_loop(0, count, done, 0)


def main_kernel(
    tab_ref,
    len_ref,
    pick_ref,
    cos_ref,
    sin_ref,
    hid_ref,
    q_hbm,
    w_ref,
    snd_ref,
    att_ref,
    pushed_ref,
    arr0,
    arr1,
    arr2,
    arr3,
    qv,
    hown,
    hl,
    hr,
    ho,
    wown,
    wsib,
    pown,
    psib,
    pget,
    kc,
    vc,
    m_ref,
    acc_ref,
    nkv,
    pbuf,
    loc_sem,
    ws_sem,
    wr_sem,
    ls_sem,
    lr_sem,
    rs_sem,
    rr_sem,
    fs_sem,
    frl_sem,
    frr_sem,
    as_sem,
    ar_sem,
    xs_sem,
    xr_sem,
    ps_sem,
    pr_sem,
):
    groups = lax.axis_size("grp")
    arrs = (arr0, arr1, arr2, arr3)
    g = lax.axis_index("grp")
    t = lax.axis_index("tp")
    chips = lax.axis_size("tp") // 2
    y = t // 2
    core = t % 2
    right = lax.rem(y + 1, chips) * 2 + core
    left = lax.rem(y + chips - 1, chips) * 2 + core
    sib = y * 2 + 1 - core
    width = hid_ref.shape[1]
    half = width // 2
    pieces = hid_ref.shape[0] // BLK
    heads = q_hbm.shape[1] // HD
    scale = math.log2(math.e) / math.sqrt(HD)

    barrier = pltpu.get_barrier_semaphore()

    def greet(k, _):
        pl.semaphore_signal(
            barrier, inc=1, device_id=(lax.rem(g + k, groups), t), device_id_type=MESH
        )
        return 0

    lax.fori_loop(1, groups, greet, 0)
    for peer in (right, left, sib):
        pl.semaphore_signal(barrier, inc=1, device_id=(g, peer), device_id_type=MESH)
    pl.semaphore_wait(barrier, groups + 2)

    own_right = []
    own_left = []
    for p in range(pieces):
        rows = pl.ds(p * BLK, BLK)
        a = remote(hid_ref.at[rows], hl.at[p], ls_sem.at[p], lr_sem.at[p], (g, right))
        b = remote(hid_ref.at[rows], hr.at[p], rs_sem.at[p], rr_sem.at[p], (g, left))
        a.start()
        b.start()
        own_right.append(a)
        own_left.append(b)

    def send_round(rho):
        def go(k, _):
            d = lax.rem(g + k, groups)
            remote(
                snd_ref.at[rho, d], arrs[rho].at[g], as_sem.at[rho], ar_sem.at[rho], (d, t)
            ).start()
            return 0

        lax.fori_loop(1, groups, go, 0)
        pltpu.make_async_copy(snd_ref.at[rho, g], arrs[rho].at[g], loc_sem.at[rho]).start()

    for rho in range(ROUNDS):
        send_round(rho)

    wcopies = []
    for i in range(chips):
        wcopies.append(
            remote(
                w_ref.at[pl.ds((2 * i + 1 - core) * width, width)],
                wsib.at[i],
                ws_sem.at[i],
                wr_sem.at[i],
                (g, sib),
            )
        )
        wcopies[-1].start()
    local = [
        pltpu.make_async_copy(q_hbm, qv, loc_sem.at[4]),
        pltpu.make_async_copy(hid_ref, hown, loc_sem.at[5]),
    ]
    for i in range(chips):
        local.append(
            pltpu.make_async_copy(
                w_ref.at[pl.ds((2 * i + core) * width, width)], wown.at[i], loc_sem.at[6 + i]
            )
        )
    for c in local:
        c.start()

    m_ref[...] = jnp.full_like(m_ref, MASKED)
    acc_ref[...] = jnp.zeros_like(acc_ref)
    for c in local:
        c.wait()
    for c in wcopies:
        c.wait()

    def project(piece, src, owner, first):
        rows = pl.ds(piece * BLK, BLK)
        x = src
        a = jnp.dot(x, wown[owner], preferred_element_type=f32)
        b = jnp.dot(x, wsib[owner], preferred_element_type=f32)
        if first:
            pown[rows, :] = a
            psib[rows, :] = b
        else:
            pown[rows, :] += a
            psib[rows, :] += b

    def own_piece(p, _):
        project(p, hown[pl.ds(p * BLK, BLK), :], y, True)
        return 0

    lax.fori_loop(0, pieces, own_piece, 0)

    at_left = lax.rem(y + chips - 1, chips)
    at_right = lax.rem(y + 1, chips)
    at_far = lax.rem(y + 2, chips)

    forwards = []
    for rho in range(ROUNDS):
        p = rho
        own_right[p].wait_recv()
        f = remote(
            hl.at[p, :, pl.ds(0, half)],
            ho.at[p, :, pl.ds(0, half)],
            fs_sem.at[p],
            frl_sem.at[p],
            (g, right),
        )
        f.start()
        forwards.append(f)
        own_left[p].wait_recv()
        f = remote(
            hr.at[p, :, pl.ds(half, half)],
            ho.at[p, :, pl.ds(half, half)],
            fs_sem.at[pieces + p],
            frr_sem.at[p],
            (g, left),
        )
        f.start()
        forwards.append(f)

        arr = arrs[rho]
        drain(arr.at[pl.ds(0, groups - 1)], ar_sem.at[rho])
        pltpu.make_async_copy(snd_ref.at[rho, g], arr.at[g], loc_sem.at[rho]).wait()

        def request(r, _, arr=arr, rho=rho):
            limit = len_ref[r]

            def place(i, _):
                code = tab_ref[r, rho * PER_ROUND + i]
                block = code // groups
                holder = code % groups
                rows = pl.ds(pl.multiple_of(i * BLK, BLK), BLK)
                live = (
                    lax.broadcasted_iota(jnp.int32, (BLK, HD), 0) + block * BLK < limit
                )
                kc[rows, 0:HD] = arr[holder, 0]
                kc[rows, HD : 2 * HD] = jnp.where(live, 0.0, MASKED).astype(bf16)
                vc[rows, 0:HD] = jnp.where(live, arr[holder, 1].astype(f32), 0.0).astype(bf16)
                vc[rows, HD : 2 * HD] = jnp.where(live, 1.0, 0.0).astype(bf16)
                return 0

            lax.fori_loop(0, PER_ROUND, place, 0)

            def step(s, _):
                scores = []
                for u in range(HEADS_PER_STEP):
                    h = s * HEADS_PER_STEP + u
                    q = qv[
                        pl.ds(pl.multiple_of(r * 2 * BLK, 2 * BLK), 2 * BLK),
                        pl.ds(pl.multiple_of(h * HD, HD), HD),
                    ]
                    q = jnp.concatenate([q, jnp.ones_like(q)], axis=1)
                    scores.append(
                        lax.dot_general(
                            q, kc[...], (((1,), (1,)), ((), ())), preferred_element_type=f32
                        )
                    )
                for u in range(HEADS_PER_STEP):
                    i = r * heads + s * HEADS_PER_STEP + u
                    old = m_ref[i]
                    new = jnp.maximum(old, jnp.max(scores[u], axis=1, keepdims=True))
                    alpha = jnp.exp2((old - new) * scale)
                    w = jnp.exp2((scores[u] - new[:, :1]) * scale).astype(bf16)
                    o = jnp.dot(w, vc[...], preferred_element_type=f32)
                    m_ref[i] = new
                    acc_ref[i, :, 0:HD] = acc_ref[i, :, 0:HD] * alpha + o[:, :HD]
                    acc_ref[i, :, HD:] = acc_ref[i, :, HD:] * alpha + o[:, HD:]
                return 0

            lax.fori_loop(0, heads // HEADS_PER_STEP, step, 0)
            return 0

        lax.fori_loop(0, 2, request, 0)
        project(p, hl[p], at_left, False)
        project(p, hr[p], at_right, False)

    exchange = []
    for p in range(pieces):
        rows = pl.ds(p * BLK, BLK)
        pltpu.make_async_copy(
            ho.at[p, :, pl.ds(0, half)], ho.at[p, :, pl.ds(0, half)], frl_sem.at[p]
        ).wait()
        pltpu.make_async_copy(
            ho.at[p, :, pl.ds(half, half)], ho.at[p, :, pl.ds(half, half)], frr_sem.at[p]
        ).wait()
        project(p, ho[p], at_far, False)
        x = remote(psib.at[rows], pget.at[rows], xs_sem.at[p], xr_sem.at[p], (g, sib))
        x.start()
        exchange.append(x)
    for p in range(pieces):
        rows = pl.ds(p * BLK, BLK)
        exchange[p].wait_recv()
        kv = pown[rows, :] + pget[rows, :]
        k = kv[:, :HD]
        k = k * cos_ref[rows, :] + pltpu.roll(k, HD // 2, 1) * sin_ref[rows, :]
        nkv[p, 0] = k.astype(bf16)
        nkv[p, 1] = kv[:, HD:].astype(bf16)

    def fill(d, _):
        pbuf[d] = nkv[pick_ref[d]]
        return 0

    lax.fori_loop(0, groups, fill, 0)

    def push(k, _):
        d = lax.rem(g + k, groups)
        remote(pbuf.at[d], pushed_ref.at[g], ps_sem, pr_sem, (d, t)).start()
        return 0

    lax.fori_loop(1, groups, push, 0)
    keep = pltpu.make_async_copy(pbuf.at[g], pushed_ref.at[g], loc_sem.at[10])
    keep.start()

    def fresh_request(r, _):
        kn = jnp.concatenate([nkv[2 * r, 0], nkv[2 * r + 1, 0]], axis=0)
        vn = jnp.concatenate([nkv[2 * r, 1], nkv[2 * r + 1, 1]], axis=0)
        vn = jnp.concatenate([vn, jnp.ones_like(vn)], axis=1)
        causal = lax.broadcasted_iota(jnp.int32, (2 * BLK, 2 * BLK), 1) <= (
            lax.broadcasted_iota(jnp.int32, (2 * BLK, 2 * BLK), 0)
        )

        def step(s, _):
            scores = []
            for u in range(HEADS_PER_STEP):
                h = s * HEADS_PER_STEP + u
                q = qv[
                    pl.ds(pl.multiple_of(r * 2 * BLK, 2 * BLK), 2 * BLK),
                    pl.ds(pl.multiple_of(h * HD, HD), HD),
                ]
                sc = lax.dot_general(
                    q, kn, (((1,), (1,)), ((), ())), preferred_element_type=f32
                )
                scores.append(jnp.where(causal, sc, MASKED))
            for u in range(HEADS_PER_STEP):
                h = s * HEADS_PER_STEP + u
                i = r * heads + h
                old = m_ref[i]
                new = jnp.maximum(old, jnp.max(scores[u], axis=1, keepdims=True))
                alpha = jnp.exp2((old - new) * scale)
                w = jnp.exp2((scores[u] - new[:, :1]) * scale).astype(bf16)
                o = jnp.dot(w, vn, preferred_element_type=f32)
                total = acc_ref[i, :, HD:] * alpha + o[:, HD:]
                value = acc_ref[i, :, 0:HD] * alpha + o[:, :HD]
                att_ref[
                    pl.ds(pl.multiple_of(r * 2 * BLK, 2 * BLK), 2 * BLK),
                    pl.ds(pl.multiple_of(h * HD, HD), HD),
                ] = (value / total).astype(bf16)
            return 0

        lax.fori_loop(0, heads // HEADS_PER_STEP, step, 0)
        return 0

    lax.fori_loop(0, 2, fresh_request, 0)

    for p in range(pieces):
        own_right[p].wait_send()
        own_left[p].wait_send()
        exchange[p].wait_send()
    for f in forwards:
        f.wait_send()
    for rho in range(ROUNDS):
        drain(snd_ref.at[rho, pl.ds(0, groups - 1)], as_sem.at[rho])
    keep.wait()
    drain(pbuf.at[pl.ds(0, groups - 1)], ps_sem)
    drain(pushed_ref.at[pl.ds(0, groups - 1)], pr_sem)


def tables(hit_holder, hit_slot, order, me, groups):
    holder = hit_holder[order].reshape(groups, 2, -1)
    slot = hit_slot[order].reshape(groups, 2, -1)
    count = holder.shape[2]
    h0 = holder[:, 0]
    earlier = jnp.arange(count)[None, :] < jnp.arange(count)[:, None]
    rank = jnp.sum(
        (holder[:, :, :, None] == holder[:, :, None, :]) & earlier[None, None], axis=-1, dtype=jnp.int32
    )
    below = jnp.sum(h0[:, None, None, :] < holder[:, :, :, None], axis=-1, dtype=jnp.int32)
    upto = jnp.sum(h0[:, None, None, :] <= holder[:, :, :, None], axis=-1, dtype=jnp.int32)
    first = (jnp.arange(2) == 0)[None, :, None]
    index = jnp.where(first, below, upto) + rank
    turn = index & 3
    place = jnp.where(first, index >> 2, holder - ((below + 3 - turn) >> 2))
    mine = (holder == me)[None] & (turn[None] == jnp.arange(ROUNDS)[:, None, None, None])
    send_rows = jnp.sum(jnp.where(mine, slot[None], 0), axis=(2, 3))
    flat = turn * PER_ROUND + place
    code = jnp.arange(count, dtype=jnp.int32) * groups + holder
    my_flat = lax.dynamic_index_in_dim(flat, me, 0, False)
    my_code = lax.dynamic_index_in_dim(code, me, 0, False)
    hit = my_flat[:, None, :] == jnp.arange(count)[None, :, None]
    table = jnp.sum(jnp.where(hit, my_code[:, None, :], 0), axis=-1)
    return send_rows.astype(jnp.int32), table.astype(jnp.int32)


def per_device(
    hidden,
    queries,
    keyval_weight,
    keyval_pool,
    prefix_len,
    slot_request,
    hit_holder,
    hit_slot,
    new_owner,
    new_slot,
):
    groups = lax.axis_size("grp")
    me = lax.axis_index("grp")
    rows, width = hidden.shape
    chips = lax.axis_size("tp") // 2
    pieces = rows // BLK
    heads = queries.shape[1] // HD
    pool_slots = keyval_pool.shape[0]
    pool = keyval_pool.reshape(pool_slots, 2, BLK, HD)
    weight = keyval_weight.reshape(-1, 2 * HD)

    my_requests = lax.dynamic_slice_in_dim(slot_request, me * 2, 2)
    lengths = prefix_len[my_requests]
    send_rows, table = tables(hit_holder, hit_slot, slot_request, me, groups)

    token = jnp.arange(rows, dtype=jnp.int32)
    positions = lengths[token // (rows // 2)] + token % (rows // 2)
    frequency = ROPE_BASE ** (-(jnp.arange(HD // 2, dtype=f32) * 2.0 / HD))
    angles = positions.astype(f32)[:, None] * frequency[None, :]
    cosine, sine = jnp.cos(angles), jnp.sin(angles)
    cosine = jnp.concatenate([cosine, cosine], axis=1)
    sine = jnp.concatenate([-sine, sine], axis=1)

    my_owner = new_owner[my_requests].reshape(-1)
    pick = jnp.sum(
        jnp.where(
            my_owner[None, :] == jnp.arange(groups)[:, None],
            jnp.arange(my_owner.shape[0], dtype=jnp.int32)[None, :],
            0,
        ),
        axis=1,
    ).astype(jnp.int32)
    all_owner = new_owner[slot_request].reshape(groups, -1)
    all_slot = new_slot[slot_request].reshape(groups, -1)
    owned = all_owner == me
    target = jnp.where(
        jnp.any(owned, axis=1), jnp.sum(jnp.where(owned, all_slot, 0), axis=1), pool_slots
    ).astype(jnp.int32)

    smem = pl.BlockSpec(memory_space=pltpu.SMEM)
    vmem = pl.BlockSpec(memory_space=pltpu.VMEM)
    anym = pl.BlockSpec(memory_space=pl.ANY)
    dma = pltpu.SemaphoreType.DMA
    V = pltpu.VMEM

    send = pl.pallas_call(
        gather_kernel,
        out_shape=jax.ShapeDtypeStruct((ROUNDS * groups, 2, BLK, HD), bf16),
        in_specs=[smem, anym],
        out_specs=anym,
        scratch_shapes=[dma],
    )(send_rows.reshape(-1), pool)
    send = send.reshape(ROUNDS, groups, 2, BLK, HD)

    attention, pushed = pl.pallas_call(
        main_kernel,
        out_shape=(
            jax.ShapeDtypeStruct(queries.shape, bf16),
            jax.ShapeDtypeStruct((groups, 2, BLK, HD), bf16),
        ),
        in_specs=[smem, smem, smem, vmem, vmem, anym, anym, anym, anym],
        out_specs=(vmem, anym),
        scratch_shapes=[V((groups, 2, BLK, HD), bf16)] * ROUNDS
        + [
            V(queries.shape, bf16),
            V((rows, width), bf16),
            V((pieces, BLK, width), bf16),
            V((pieces, BLK, width), bf16),
            V((pieces, BLK, width), bf16),
            V((chips, width, 2 * HD), bf16),
            V((chips, width, 2 * HD), bf16),
            V((rows, 2 * HD), f32),
            V((rows, 2 * HD), f32),
            V((rows, 2 * HD), f32),
            V((PER_ROUND * BLK, 2 * HD), bf16),
            V((PER_ROUND * BLK, 2 * HD), bf16),
            V((2 * heads, 2 * BLK, HD), f32),
            V((2 * heads, 2 * BLK, 2 * HD), f32),
            V((pieces, 2, BLK, HD), bf16),
            V((groups, 2, BLK, HD), bf16),
            dma((11,)),
            dma((chips,)),
            dma((chips,)),
            dma((pieces,)),
            dma((pieces,)),
            dma((pieces,)),
            dma((pieces,)),
            dma((2 * pieces,)),
            dma((pieces,)),
            dma((pieces,)),
            dma((ROUNDS,)),
            dma((ROUNDS,)),
            dma((pieces,)),
            dma((pieces,)),
            dma,
            dma,
        ],
        compiler_params=pltpu.CompilerParams(
            collective_id=0, has_side_effects=True, vmem_limit_bytes=60 * 2**20
        ),
    )(table, lengths, pick, cosine, sine, hidden, queries, weight, send)

    new_pool = pl.pallas_call(
        patch_kernel,
        out_shape=jax.ShapeDtypeStruct(pool.shape, bf16),
        in_specs=[smem, anym, anym],
        out_specs=anym,
        scratch_shapes=[dma((groups,))],
        input_output_aliases={1: 0},
    )(target, pool, pushed)
    return attention, new_pool.reshape(keyval_pool.shape)


def solution(mesh):
    in_specs = (
        P("grp", "tp"),
        P("grp", "tp"),
        P(None, None, "tp"),
        P("grp", None, "tp", None, None),
        P(),
        P(),
        P(),
        P(),
        P(),
        P(),
    )
    out_specs = (P("grp", "tp"), P("grp", None, "tp", None, None))
    return jax.shard_map(
        per_device, mesh=mesh, in_specs=in_specs, out_specs=out_specs, check_vma=False
    )
```

```python
import functools
import math

import jax
import jax.numpy as jnp
import numpy as np
from jax import lax
from jax.experimental import pallas as pl
from jax.experimental.pallas import tpu as pltpu
from jax.sharding import PartitionSpec as P

MESH = pl.DeviceIdType.MESH
ROPE_BASE = 1000000.0
MASKED = -1e30
BLK = 128
HD = 128
ROUNDS = 4
PER_ROUND = 8
HEADS_PER_STEP = 6
MAXB = 32
WIDE = 512
bf16 = jnp.bfloat16
f32 = jnp.float32


def remote(src, dst, send_sem, recv_sem, device):
    return pltpu.make_async_remote_copy(
        src_ref=src,
        dst_ref=dst,
        send_sem=send_sem,
        recv_sem=recv_sem,
        device_id=device,
        device_id_type=MESH,
    )


def drain(ref, sem):
    pltpu.make_async_copy(ref, ref, sem).wait()


def store_kernel(
    request_ref, owner_ref, slot_ref, pool_ref, pushed_ref, out_ref, pool, pushed, in_sem, out_sem, push_sem, row_sem
):
    count = pushed_ref.shape[0]
    limit = out_ref.shape[0]
    parts = in_sem.shape[0]
    size = limit // parts
    me = lax.axis_index("grp")
    loads = [
        pltpu.make_async_copy(
            pool_ref.at[pl.ds(i * size, size)], pool.at[pl.ds(i * size, size)], in_sem.at[i]
        )
        for i in range(parts)
    ]
    stores = [
        pltpu.make_async_copy(
            pool.at[pl.ds(i * size, size)], out_ref.at[pl.ds(i * size, size)], out_sem.at[i]
        )
        for i in range(parts)
    ]
    fetch = pltpu.make_async_copy(pushed_ref, pushed, push_sem)
    for c in loads:
        c.start()
    fetch.start()

    def target(i):
        row = limit
        for r in range(2):
            n = request_ref[2 * i + r]
            for c in range(2):
                row = jnp.where(owner_ref[c, n] == me, slot_ref[c, n], row)
        return row

    for i in range(parts):
        loads[i].wait()
        stores[i].start()
    fetch.wait()
    for c in stores:
        c.wait()

    def go(i, _):
        row = target(i)

        @pl.when(row < limit)
        def _():
            pltpu.make_async_copy(pushed.at[i], out_ref.at[row], row_sem.at[i]).start()

        return 0

    def done(i, _):
        row = target(i)

        @pl.when(row < limit)
        def _():
            pltpu.make_async_copy(pushed.at[i], out_ref.at[row], row_sem.at[i]).wait()

        return 0

    lax.fori_loop(0, count, go, 0)
    lax.fori_loop(0, count, done, 0)


def running_count(marks):
    lane = lax.broadcasted_iota(jnp.int32, marks.shape, 1)
    total = marks
    for shift in (1, 2, 4, 8, 16):
        total = total + jnp.where(lane >= shift, pltpu.roll(total, shift, 1), 0)
    return total - marks


def rows_to_send(h0, h1, s0, s1, me):
    e0 = (h0 == me).astype(jnp.int32)
    e1 = (h1 == me).astype(jnp.int32)
    start = jnp.sum(((h0 >= 0) & (h0 < me)).astype(jnp.int32), axis=1, keepdims=True)
    mine = jnp.sum(e0, axis=1, keepdims=True)
    turn0 = (running_count(e0) + start) & (ROUNDS - 1)
    turn1 = (running_count(e1) + (start + mine)) & (ROUNDS - 1)
    lane = lax.broadcasted_iota(jnp.int32, h0.shape, 1)
    rows = jnp.zeros_like(h0)
    for rho in range(ROUNDS):
        chosen = jnp.where((e0 == 1) & (turn0 == rho), s0, 0) + jnp.where(
            (e1 == 1) & (turn1 == rho), s1, 0
        )
        rows = jnp.where(lane == rho, jnp.sum(chosen, axis=1, keepdims=True), rows)
    return rows


def blocks_to_read(h0, h1, groups):
    count = MAXB
    sub = lax.broadcasted_iota(jnp.int32, (count, HD), 0)
    lane = lax.broadcasted_iota(jnp.int32, (count, HD), 1)
    inside = lane < count
    eye = sub == lane
    h0 = jnp.broadcast_to(h0, (count, HD))
    h1 = jnp.broadcast_to(h1, (count, HD))
    h0_col = jnp.sum(jnp.where(eye, h0, 0), axis=1, keepdims=True)
    h1_col = jnp.sum(jnp.where(eye, h1, 0), axis=1, keepdims=True)

    def over_rows(mark):
        return jnp.sum(mark.astype(jnp.int32), axis=0, keepdims=True)

    rank0 = over_rows((h0_col == h0) & (sub < lane))
    rank1 = over_rows((h1_col == h1) & (sub < lane))
    below0 = over_rows(h0_col < h0)
    below1 = over_rows(h0_col < h1)
    upto1 = over_rows(h0_col <= h1)
    index0 = below0 + rank0
    place0 = (index0 & (ROUNDS - 1)) * PER_ROUND + (index0 >> 2)
    turn1 = (upto1 + rank1) & (ROUNDS - 1)
    place1 = turn1 * PER_ROUND + h1[0:1] - ((below1 + (ROUNDS - 1) - turn1) >> 2)
    code0 = lane * groups + h0
    code1 = lane * groups + h1
    col0 = jnp.sum(jnp.where((place0 == sub) & inside, code0, 0), axis=1, keepdims=True)
    col1 = jnp.sum(jnp.where((place1 == sub) & inside, code1, 0), axis=1, keepdims=True)
    return jnp.where(lane == 0, col0, jnp.where(lane == 1, col1, 0))


def main_kernel(
    request_ref,
    length_ref,
    owner_ref,
    freq_ref,
    holder_ref,
    slot_ref,
    hid_ref,
    q_hbm,
    w_ref,
    pool_ref,
    att_ref,
    pushed_ref,
    arr0,
    arr1,
    arr2,
    arr3,
    pool,
    sbuf,
    hs,
    tab_v,
    tab,
    qv,
    hown,
    hl,
    hr,
    ho,
    wraw_own,
    wraw_sib,
    wide,
    wown,
    wsib,
    pown,
    psib,
    pget,
    kc,
    vc,
    m_ref,
    acc_ref,
    nkv,
    pbuf,
    loc_sem,
    ws_sem,
    wr_sem,
    ls_sem,
    lr_sem,
    rs_sem,
    rr_sem,
    fs_sem,
    frl_sem,
    frr_sem,
    as_sem,
    ar_sem,
    xs_sem,
    xr_sem,
    ps_sem,
    pr_sem,
):
    groups = lax.axis_size("grp")
    arrs = (arr0, arr1, arr2, arr3)
    g = lax.axis_index("grp")
    t = lax.axis_index("tp")
    chips = lax.axis_size("tp") // 2
    y = t // 2
    core = t % 2
    right = lax.rem(y + 1, chips) * 2 + core
    left = lax.rem(y + chips - 1, chips) * 2 + core
    sib = y * 2 + 1 - core
    width = hid_ref.shape[1]
    half = width // 2
    pieces = hid_ref.shape[0] // BLK
    heads = q_hbm.shape[1] // HD
    scale = math.log2(math.e) / math.sqrt(HD)

    local = [
        pltpu.make_async_copy(pool_ref, pool, loc_sem.at[0]),
        pltpu.make_async_copy(hid_ref, hown, loc_sem.at[1]),
        pltpu.make_async_copy(q_hbm, qv, loc_sem.at[2]),
    ]
    for i in range(chips):
        local.append(
            pltpu.make_async_copy(
                w_ref.at[pl.ds((2 * i + core) * (2 * width), 2 * width)],
                wraw_own.at[i],
                loc_sem.at[3 + i],
            )
        )
    for c in local:
        c.start()

    barrier = pltpu.get_barrier_semaphore()

    def greet(k, _):
        pl.semaphore_signal(
            barrier, inc=1, device_id=(lax.rem(g + k, groups), t), device_id_type=MESH
        )
        return 0

    lax.fori_loop(1, groups, greet, 0)
    for peer in (right, left, sib):
        pl.semaphore_signal(barrier, inc=1, device_id=(g, peer), device_id_type=MESH)
    pl.semaphore_wait(barrier, groups + 2)

    own_right = []
    own_left = []
    for p in range(pieces):
        rows = pl.ds(p * BLK, BLK)
        a = remote(hid_ref.at[rows], hl.at[p], ls_sem.at[p], lr_sem.at[p], (g, right))
        b = remote(hid_ref.at[rows], hr.at[p], rs_sem.at[p], rr_sem.at[p], (g, left))
        a.start()
        b.start()
        own_right.append(a)
        own_left.append(b)

    wcopies = []
    for i in range(chips):
        wcopies.append(
            remote(
                w_ref.at[pl.ds((2 * i + 1 - core) * (2 * width), 2 * width)],
                wraw_sib.at[i],
                ws_sem.at[i],
                wr_sem.at[i],
                (g, sib),
            )
        )
        wcopies[-1].start()

    hs[...] = jnp.full_like(hs, -1)

    def in_order(i, _):
        for r in range(2):
            n = request_ref[2 * i + r]
            hs[r, pl.ds(i, 1), 0:MAXB] = holder_ref[pl.ds(n, 1), :]
            hs[2 + r, pl.ds(i, 1), 0:MAXB] = slot_ref[pl.ds(n, 1), :]
        return 0

    lax.fori_loop(0, groups, in_order, 0)
    tab_v[0:groups] = rows_to_send(hs[0], hs[1], hs[2], hs[3], g)
    tab_v[groups:] = blocks_to_read(hs[0, pl.ds(g, 1), :], hs[1, pl.ds(g, 1), :], groups)
    to_smem = pltpu.make_async_copy(tab_v, tab, loc_sem.at[3 + chips])
    to_smem.start()
    to_smem.wait()
    n0 = request_ref[2 * g]
    n1 = request_ref[2 * g + 1]
    len0 = length_ref[n0]
    len1 = length_ref[n1]

    local[0].wait()
    for rho in range(ROUNDS):
        arr = arrs[rho]

        def fill(k, _, rho=rho, arr=arr):
            d = lax.rem(g + k, groups)
            sbuf[rho, d] = pool[tab[d, rho]]
            remote(sbuf.at[rho, d], arr.at[g], as_sem.at[rho], ar_sem.at[rho], (d, t)).start()
            return 0

        lax.fori_loop(1, groups, fill, 0)
        arr[g] = pool[tab[g, rho]]

    m_ref[...] = jnp.full_like(m_ref, MASKED)
    acc_ref[...] = jnp.zeros_like(acc_ref)

    def unpack(raw, out, i):
        part = WIDE

        def go(j, _):
            wide[0:part] = raw[i, pl.ds(pl.multiple_of(j * part, part), part), :].astype(f32)
            rows = pl.ds(pl.multiple_of(j * (part // 2), part // 2), part // 2)
            out[i, rows, 0:HD] = wide[pl.ds(0, part // 2, stride=2), :].astype(bf16)
            out[i, rows, HD:] = wide[pl.ds(1, part // 2, stride=2), :].astype(bf16)
            return 0

        lax.fori_loop(0, 2 * width // part, go, 0)

    def project(piece, x, owner, first):
        rows = pl.ds(piece * BLK, BLK)
        a = jnp.dot(x, wown[owner], preferred_element_type=f32)
        b = jnp.dot(x, wsib[owner], preferred_element_type=f32)
        if first:
            pown[rows, :] = a
            psib[rows, :] = b
        else:
            pown[rows, :] += a
            psib[rows, :] += b

    at_left = lax.rem(y + chips - 1, chips)
    at_right = lax.rem(y + 1, chips)
    at_far = lax.rem(y + 2, chips)
    forwards = []

    def forward(p):
        own_right[p].wait_recv()
        f = remote(
            hl.at[p, :, pl.ds(0, half)],
            ho.at[p, :, pl.ds(0, half)],
            fs_sem.at[p],
            frl_sem.at[p],
            (g, right),
        )
        f.start()
        forwards.append(f)
        own_left[p].wait_recv()
        f = remote(
            hr.at[p, :, pl.ds(half, half)],
            ho.at[p, :, pl.ds(half, half)],
            fs_sem.at[pieces + p],
            frr_sem.at[p],
            (g, left),
        )
        f.start()
        forwards.append(f)

    def far(p):
        for cols, sem in ((pl.ds(0, half), frl_sem), (pl.ds(half, half), frr_sem)):
            pltpu.make_async_copy(ho.at[p, :, cols], ho.at[p, :, cols], sem.at[p]).wait()
        project(p, ho[p], at_far, False)

    def attend(rho, r):
        arr = arrs[rho]
        limit = (len0, len1)[r]

        def place(i, _):
            code = tab[groups + rho * PER_ROUND + i, r]
            block = code // groups
            holder = code % groups
            rows = pl.ds(pl.multiple_of(i * BLK, BLK), BLK)
            live = lax.broadcasted_iota(jnp.int32, (BLK, HD), 0) + block * BLK < limit
            kc[rows, 0:HD] = arr[holder, 0]
            kc[rows, HD : 2 * HD] = jnp.where(live, 0.0, MASKED).astype(bf16)
            vc[rows, 0:HD] = jnp.where(live, arr[holder, 1].astype(f32), 0.0).astype(bf16)
            vc[rows, HD : 2 * HD] = jnp.where(live, 1.0, 0.0).astype(bf16)
            return 0

        lax.fori_loop(0, PER_ROUND, place, 0)

        def step(s, _):
            scores = []
            for u in range(HEADS_PER_STEP):
                h = s * HEADS_PER_STEP + u
                q = qv[r * 2 * BLK : (r + 1) * 2 * BLK, pl.ds(pl.multiple_of(h * HD, HD), HD)]
                q = jnp.concatenate([q, jnp.ones_like(q)], axis=1)
                scores.append(
                    lax.dot_general(
                        q, kc[...], (((1,), (1,)), ((), ())), preferred_element_type=f32
                    )
                )
            for u in range(HEADS_PER_STEP):
                i = r * heads + s * HEADS_PER_STEP + u
                old = m_ref[i]
                new = jnp.maximum(old, jnp.max(scores[u], axis=1, keepdims=True))
                alpha = jnp.exp2((old - new) * scale)
                w = jnp.exp2((scores[u] - new[:, :1]) * scale).astype(bf16)
                o = jnp.dot(w, vc[...], preferred_element_type=f32)
                m_ref[i] = new
                acc_ref[i, :, 0:HD] = acc_ref[i, :, 0:HD] * alpha + o[:, :HD]
                acc_ref[i, :, HD:] = acc_ref[i, :, HD:] * alpha + o[:, HD:]
            return 0

        lax.fori_loop(0, heads // HEADS_PER_STEP, step, 0)

    def arrived(rho):
        drain(arrs[rho].at[pl.ds(0, groups - 1)], ar_sem.at[rho])

    for c in local[3:]:
        c.wait()

    def own_weights(i, _):
        unpack(wraw_own, wown, i)
        return 0

    lax.fori_loop(0, chips, own_weights, 0)
    local[1].wait()
    local[2].wait()
    forward(0)
    for c in wcopies:
        c.wait()

    def swapped_weights(i, _):
        unpack(wraw_sib, wsib, i)
        return 0

    lax.fori_loop(0, chips, swapped_weights, 0)

    arrived(0)
    attend(0, 0)
    forward(1)
    attend(0, 1)

    def own_piece(p, _):
        project(p, hown[pl.ds(p * BLK, BLK), :], y, True)
        return 0

    lax.fori_loop(0, pieces, own_piece, 0)
    project(0, hl[0], at_left, False)
    project(0, hr[0], at_right, False)
    forward(2)
    arrived(1)
    attend(1, 0)
    project(1, hl[1], at_left, False)
    project(1, hr[1], at_right, False)
    forward(3)
    attend(1, 1)
    for p in (2, 3):
        project(p, hl[p], at_left, False)
        project(p, hr[p], at_right, False)
    arrived(2)
    attend(2, 0)
    attend(2, 1)

    exchange = []
    for p in range(pieces):
        rows = pl.ds(p * BLK, BLK)
        far(p)
        x = remote(psib.at[rows], pget.at[rows], xs_sem.at[p], xr_sem.at[p], (g, sib))
        x.start()
        exchange.append(x)

    row = lax.broadcasted_iota(jnp.int32, (BLK, HD), 0)
    lane = lax.broadcasted_iota(jnp.int32, (BLK, HD), 1)
    for p in range(pieces):
        rows = pl.ds(p * BLK, BLK)
        angle = (row + ((len0, len1)[p // 2] + (p % 2) * BLK)).astype(f32) * freq_ref[...]
        cosine = jnp.cos(angle)
        sine = jnp.where(lane < HD // 2, -1.0, 1.0) * jnp.sin(angle)
        exchange[p].wait_recv()
        kv = pown[rows, :] + pget[rows, :]
        k = kv[:, :HD]
        k = k * cosine + pltpu.roll(k, HD // 2, 1) * sine
        nkv[p, 0] = k.astype(bf16)
        nkv[p, 1] = kv[:, HD:].astype(bf16)

    owners = [owner_ref[c, n] for n in (n0, n1) for c in range(2)]

    def choose(d):
        block = 0
        for e in range(1, len(owners)):
            block = jnp.where(owners[e] == d, e, block)
        return block

    def push(k, _):
        d = lax.rem(g + k, groups)
        pbuf[d] = nkv[choose(d)]
        remote(pbuf.at[d], pushed_ref.at[g], ps_sem, pr_sem, (d, t)).start()
        return 0

    lax.fori_loop(1, groups, push, 0)
    pbuf[g] = nkv[choose(g)]
    keep = pltpu.make_async_copy(pbuf.at[g], pushed_ref.at[g], loc_sem.at[4 + chips])
    keep.start()

    arrived(3)
    attend(3, 0)
    attend(3, 1)

    def fresh_request(r, _):
        kn = jnp.concatenate([nkv[2 * r, 0], nkv[2 * r + 1, 0]], axis=0)
        vn = jnp.concatenate([nkv[2 * r, 1], nkv[2 * r + 1, 1]], axis=0)
        vn = jnp.concatenate([vn, jnp.ones_like(vn)], axis=1)
        causal = lax.broadcasted_iota(jnp.int32, (2 * BLK, 2 * BLK), 1) <= (
            lax.broadcasted_iota(jnp.int32, (2 * BLK, 2 * BLK), 0)
        )

        def step(s, _):
            scores = []
            for u in range(HEADS_PER_STEP):
                h = s * HEADS_PER_STEP + u
                q = qv[
                    pl.ds(pl.multiple_of(r * 2 * BLK, 2 * BLK), 2 * BLK),
                    pl.ds(pl.multiple_of(h * HD, HD), HD),
                ]
                sc = lax.dot_general(
                    q, kn, (((1,), (1,)), ((), ())), preferred_element_type=f32
                )
                scores.append(jnp.where(causal, sc, MASKED))
            for u in range(HEADS_PER_STEP):
                h = s * HEADS_PER_STEP + u
                i = r * heads + h
                old = m_ref[i]
                new = jnp.maximum(old, jnp.max(scores[u], axis=1, keepdims=True))
                alpha = jnp.exp2((old - new) * scale)
                w = jnp.exp2((scores[u] - new[:, :1]) * scale).astype(bf16)
                o = jnp.dot(w, vn, preferred_element_type=f32)
                total = acc_ref[i, :, HD:] * alpha + o[:, HD:]
                value = acc_ref[i, :, 0:HD] * alpha + o[:, :HD]
                att_ref[
                    pl.ds(pl.multiple_of(r * 2 * BLK, 2 * BLK), 2 * BLK),
                    pl.ds(pl.multiple_of(h * HD, HD), HD),
                ] = (value / total).astype(bf16)
            return 0

        lax.fori_loop(0, heads // HEADS_PER_STEP, step, 0)
        return 0

    lax.fori_loop(0, 2, fresh_request, 0)

    for p in range(pieces):
        own_right[p].wait_send()
        own_left[p].wait_send()
        exchange[p].wait_send()
    for f in forwards:
        f.wait_send()
    for rho in range(ROUNDS):
        drain(sbuf.at[rho, pl.ds(0, groups - 1)], as_sem.at[rho])
    keep.wait()
    drain(pbuf.at[pl.ds(0, groups - 1)], ps_sem)
    drain(pushed_ref.at[pl.ds(0, groups - 1)], pr_sem)


def per_device(
    hidden,
    queries,
    keyval_weight,
    keyval_pool,
    prefix_len,
    slot_request,
    hit_holder,
    hit_slot,
    new_owner,
    new_slot,
):
    groups = lax.axis_size("grp")
    rows, width = hidden.shape
    chips = lax.axis_size("tp") // 2
    pieces = rows // BLK
    heads = queries.shape[1] // HD
    pool_slots = keyval_pool.shape[0]
    pool = keyval_pool.reshape(pool_slots, 2, BLK, HD)
    weight = keyval_weight.reshape(-1, HD)

    frequency = ROPE_BASE ** (-(np.arange(HD // 2) * 2.0 / HD))
    frequency = jnp.asarray(np.concatenate([frequency, frequency])[None, :], f32)

    smem = pl.BlockSpec(memory_space=pltpu.SMEM)
    vmem = pl.BlockSpec(memory_space=pltpu.VMEM)
    anym = pl.BlockSpec(memory_space=pl.ANY)
    dma = pltpu.SemaphoreType.DMA
    V = pltpu.VMEM

    attention, pushed = pl.pallas_call(
        main_kernel,
        out_shape=(
            jax.ShapeDtypeStruct(queries.shape, bf16),
            jax.ShapeDtypeStruct((groups, 2, BLK, HD), bf16),
        ),
        in_specs=[smem, smem, smem, vmem, vmem, vmem, anym, anym, anym, anym],
        out_specs=(vmem, anym),
        scratch_shapes=[V((groups, 2, BLK, HD), bf16)] * ROUNDS
        + [
            V(pool.shape, bf16),
            V((ROUNDS, groups, 2, BLK, HD), bf16),
            V((4, groups, HD), jnp.int32),
            V((groups + MAXB, HD), jnp.int32),
            pltpu.SMEM((groups + MAXB, HD), jnp.int32),
            V(queries.shape, bf16),
            V((rows, width), bf16),
            V((pieces, BLK, width), bf16),
            V((pieces, BLK, width), bf16),
            V((pieces, BLK, width), bf16),
            V((chips, 2 * width, HD), bf16),
            V((chips, 2 * width, HD), bf16),
            V((WIDE + 8, HD), f32),
            V((chips, width, 2 * HD), bf16),
            V((chips, width, 2 * HD), bf16),
            V((rows, 2 * HD), f32),
            V((rows, 2 * HD), f32),
            V((rows, 2 * HD), f32),
            V((PER_ROUND * BLK, 2 * HD), bf16),
            V((PER_ROUND * BLK, 2 * HD), bf16),
            V((2 * heads, 2 * BLK, HD), f32),
            V((2 * heads, 2 * BLK, 2 * HD), f32),
            V((pieces, 2, BLK, HD), bf16),
            V((groups, 2, BLK, HD), bf16),
            dma((5 + chips,)),
            dma((chips,)),
            dma((chips,)),
            dma((pieces,)),
            dma((pieces,)),
            dma((pieces,)),
            dma((pieces,)),
            dma((2 * pieces,)),
            dma((pieces,)),
            dma((pieces,)),
            dma((ROUNDS,)),
            dma((ROUNDS,)),
            dma((pieces,)),
            dma((pieces,)),
            dma,
            dma,
        ],
        compiler_params=pltpu.CompilerParams(
            collective_id=0, has_side_effects=True, vmem_limit_bytes=62 * 2**20
        ),
    )(
        slot_request,
        prefix_len,
        new_owner.T,
        frequency,
        hit_holder,
        hit_slot,
        hidden,
        queries,
        weight,
        pool,
    )

    parts = 5
    new_pool = pl.pallas_call(
        store_kernel,
        out_shape=jax.ShapeDtypeStruct(pool.shape, bf16),
        in_specs=[smem, smem, smem, anym, anym],
        out_specs=anym,
        scratch_shapes=[
            V(pool.shape, bf16),
            V((groups, 2, BLK, HD), bf16),
            dma((parts,)),
            dma((parts,)),
            dma,
            dma((groups,)),
        ],
        compiler_params=pltpu.CompilerParams(vmem_limit_bytes=62 * 2**20),
    )(slot_request, new_owner.T, new_slot.T, pool, pushed)
    return attention, new_pool.reshape(keyval_pool.shape)


def solution(mesh):
    in_specs = (
        P("grp", "tp"),
        P("grp", "tp"),
        P(None, None, "tp"),
        P("grp", None, "tp", None, None),
        P(),
        P(),
        P(),
        P(),
        P(),
        P(),
    )
    out_specs = (P("grp", "tp"), P("grp", None, "tp", None, None))
    return jax.shard_map(
        per_device, mesh=mesh, in_specs=in_specs, out_specs=out_specs, check_vma=False
    )
```

```python
import functools
import math

import jax
import jax.numpy as jnp
import numpy as np
from jax import lax
from jax.experimental import pallas as pl
from jax.experimental.pallas import tpu as pltpu
from jax.sharding import PartitionSpec as P

MESH = pl.DeviceIdType.MESH
ROPE_BASE = 1000000.0
MASKED = -1e30
BLK = 128
HD = 128
ROUNDS = 4
PER_ROUND = 8
HEADS_PER_STEP = 6
MAXB = 32
WIDE = 512
STRIP = 32
AHEAD = 2
bf16 = jnp.bfloat16
f32 = jnp.float32


def remote(src, dst, send_sem, recv_sem, device):
    return pltpu.make_async_remote_copy(
        src_ref=src,
        dst_ref=dst,
        send_sem=send_sem,
        recv_sem=recv_sem,
        device_id=device,
        device_id_type=MESH,
    )


def drain(ref, sem):
    pltpu.make_async_copy(ref, ref, sem).wait()


def store_kernel(
    request_ref, owner_ref, slot_ref, pool_ref, pushed_ref, out_ref, pool, pushed, in_sem, out_sem, push_sem
):
    count = pushed_ref.shape[0]
    limit = out_ref.shape[0]
    parts = in_sem.shape[0]
    size = limit // parts
    me = lax.axis_index("grp")
    loads = [
        pltpu.make_async_copy(
            pool_ref.at[pl.ds(i * size, size)], pool.at[pl.ds(i * size, size)], in_sem.at[i]
        )
        for i in range(parts)
    ]
    stores = [
        pltpu.make_async_copy(
            pool.at[pl.ds(i * size, size)], out_ref.at[pl.ds(i * size, size)], out_sem.at[i]
        )
        for i in range(parts)
    ]
    fetch = pltpu.make_async_copy(pushed_ref, pushed, push_sem)
    for c in loads:
        c.start()
    fetch.start()

    def target(i):
        row = limit
        for r in range(2):
            n = request_ref[2 * i + r]
            for c in range(2):
                row = jnp.where(owner_ref[c, n] == me, slot_ref[c, n], row)
        return row

    for c in loads:
        c.wait()
    fetch.wait()

    def patch(i, _):
        row = target(i)

        @pl.when(row < limit)
        def _():
            pool[row] = pushed[i]

        return 0

    lax.fori_loop(0, count, patch, 0)
    for c in stores:
        c.start()
    for c in stores:
        c.wait()


def running_count(marks):
    lane = lax.broadcasted_iota(jnp.int32, marks.shape, 1)
    total = marks
    for shift in (1, 2, 4, 8, 16):
        total = total + jnp.where(lane >= shift, pltpu.roll(total, shift, 1), 0)
    return total - marks


def rows_to_send(h0, h1, s0, s1, me):
    e0 = (h0 == me).astype(jnp.int32)
    e1 = (h1 == me).astype(jnp.int32)
    start = jnp.sum(((h0 >= 0) & (h0 < me)).astype(jnp.int32), axis=1, keepdims=True)
    mine = jnp.sum(e0, axis=1, keepdims=True)
    turn0 = (running_count(e0) + start) & (ROUNDS - 1)
    turn1 = (running_count(e1) + (start + mine)) & (ROUNDS - 1)
    lane = lax.broadcasted_iota(jnp.int32, h0.shape, 1)
    rows = jnp.zeros_like(h0)
    for rho in range(ROUNDS):
        chosen = jnp.where((e0 == 1) & (turn0 == rho), s0, 0) + jnp.where(
            (e1 == 1) & (turn1 == rho), s1, 0
        )
        rows = jnp.where(lane == rho, jnp.sum(chosen, axis=1, keepdims=True), rows)
    return rows


def blocks_to_read(h0, h1, groups):
    count = MAXB
    sub = lax.broadcasted_iota(jnp.int32, (count, HD), 0)
    lane = lax.broadcasted_iota(jnp.int32, (count, HD), 1)
    inside = lane < count
    eye = sub == lane
    h0 = jnp.broadcast_to(h0, (count, HD))
    h1 = jnp.broadcast_to(h1, (count, HD))
    h0_col = jnp.sum(jnp.where(eye, h0, 0), axis=1, keepdims=True)
    h1_col = jnp.sum(jnp.where(eye, h1, 0), axis=1, keepdims=True)

    def over_rows(mark):
        return jnp.sum(mark.astype(jnp.int32), axis=0, keepdims=True)

    rank0 = over_rows((h0_col == h0) & (sub < lane))
    rank1 = over_rows((h1_col == h1) & (sub < lane))
    below0 = over_rows(h0_col < h0)
    below1 = over_rows(h0_col < h1)
    upto1 = over_rows(h0_col <= h1)
    index0 = below0 + rank0
    place0 = (index0 & (ROUNDS - 1)) * PER_ROUND + (index0 >> 2)
    turn1 = (upto1 + rank1) & (ROUNDS - 1)
    place1 = turn1 * PER_ROUND + h1[0:1] - ((below1 + (ROUNDS - 1) - turn1) >> 2)
    code0 = lane * groups + h0
    code1 = lane * groups + h1
    col0 = jnp.sum(jnp.where((place0 == sub) & inside, code0, 0), axis=1, keepdims=True)
    col1 = jnp.sum(jnp.where((place1 == sub) & inside, code1, 0), axis=1, keepdims=True)
    return jnp.where(lane == 0, col0, jnp.where(lane == 1, col1, 0))


def main_kernel(
    request_ref,
    length_ref,
    owner_ref,
    freq_ref,
    holder_ref,
    slot_ref,
    hid_ref,
    q_hbm,
    w_ref,
    pool_ref,
    att_ref,
    pushed_ref,
    arr0,
    arr1,
    arr2,
    arr3,
    pool,
    sbuf,
    hs,
    tab_v,
    tab,
    qv,
    hown,
    hl,
    hr,
    ho,
    wraw_own,
    wraw_sib,
    wide,
    wown,
    wsib,
    pown,
    psib,
    pget,
    kc,
    vc,
    m_ref,
    acc_ref,
    nkv,
    pbuf,
    loc_sem,
    ws_sem,
    wr_sem,
    ls_sem,
    lr_sem,
    rs_sem,
    rr_sem,
    fs_sem,
    frl_sem,
    frr_sem,
    as_sem,
    ar_sem,
    xs_sem,
    xr_sem,
    ps_sem,
    pr_sem,
):
    groups = lax.axis_size("grp")
    arrs = (arr0, arr1, arr2, arr3)
    g = lax.axis_index("grp")
    t = lax.axis_index("tp")
    chips = lax.axis_size("tp") // 2
    y = t // 2
    core = t % 2
    right = lax.rem(y + 1, chips) * 2 + core
    left = lax.rem(y + chips - 1, chips) * 2 + core
    sib = y * 2 + 1 - core
    blocks, _, width = hid_ref.shape
    half = width // 2
    pieces = BLK // STRIP
    size = blocks * STRIP
    heads = q_hbm.shape[1] // HD
    scale = math.log2(math.e) / math.sqrt(HD)

    local = [
        pltpu.make_async_copy(pool_ref, pool, loc_sem.at[0]),
        pltpu.make_async_copy(hid_ref, hown, loc_sem.at[1]),
        pltpu.make_async_copy(q_hbm, qv, loc_sem.at[2]),
    ]
    for i in range(chips):
        local.append(
            pltpu.make_async_copy(
                w_ref.at[pl.ds((2 * i + core) * (2 * width), 2 * width)],
                wraw_own.at[i],
                loc_sem.at[3 + i],
            )
        )
    local[0].start()

    barrier = pltpu.get_barrier_semaphore()

    def greet(k, _):
        pl.semaphore_signal(
            barrier, inc=1, device_id=(lax.rem(g + k, groups), t), device_id_type=MESH
        )
        return 0

    lax.fori_loop(1, groups, greet, 0)
    for peer in (right, left, sib):
        pl.semaphore_signal(barrier, inc=1, device_id=(g, peer), device_id_type=MESH)
    hs[...] = jnp.full_like(hs, -1)

    def in_order(i, _):
        for r in range(2):
            n = request_ref[2 * i + r]
            hs[r, pl.ds(i, 1), 0:MAXB] = holder_ref[pl.ds(n, 1), :]
            hs[2 + r, pl.ds(i, 1), 0:MAXB] = slot_ref[pl.ds(n, 1), :]
        return 0

    lax.fori_loop(0, groups, in_order, 0)
    tab_v[0:groups] = rows_to_send(hs[0], hs[1], hs[2], hs[3], g)
    tab_v[groups:] = blocks_to_read(hs[0, pl.ds(g, 1), :], hs[1, pl.ds(g, 1), :], groups)
    to_smem = pltpu.make_async_copy(tab_v, tab, loc_sem.at[3 + chips])
    to_smem.start()
    pl.semaphore_wait(barrier, groups + 2)

    own_right = []
    own_left = []
    for p in range(pieces):
        strip = hid_ref.at[:, pl.ds(p * STRIP, STRIP)]
        own_right.append(remote(strip, hl.at[p], ls_sem.at[p], lr_sem.at[p], (g, right)))
        own_left.append(remote(strip, hr.at[p], rs_sem.at[p], rr_sem.at[p], (g, left)))
    for p in range(AHEAD):
        own_right[p].start()
        own_left[p].start()

    to_smem.wait()
    n0 = request_ref[2 * g]
    n1 = request_ref[2 * g + 1]
    len0 = length_ref[n0]
    len1 = length_ref[n1]

    local[0].wait()
    for rho in range(ROUNDS):
        arr = arrs[rho]

        def fill(k, _, rho=rho, arr=arr):
            d = lax.rem(g + k, groups)
            sbuf[rho, d] = pool[tab[d, rho]]
            remote(sbuf.at[rho, d], arr.at[g], as_sem.at[rho], ar_sem.at[rho], (d, t)).start()
            return 0

        lax.fori_loop(1, groups, fill, 0)
        arr[g] = pool[tab[g, rho]]

    wcopies = []
    for i in range(chips):
        wcopies.append(
            remote(
                w_ref.at[pl.ds((2 * i + 1 - core) * (2 * width), 2 * width)],
                wraw_sib.at[i],
                ws_sem.at[i],
                wr_sem.at[i],
                (g, sib),
            )
        )
        wcopies[-1].start()

    for c in local[1:]:
        c.start()
    ml_lane = lax.broadcasted_iota(jnp.int32, (2 * BLK, HD), 1) < HD // 2
    m_ref[...] = jnp.where(
        lax.broadcasted_iota(jnp.int32, m_ref.shape, 2) < HD // 2, MASKED, 0.0
    )
    acc_ref[...] = jnp.zeros_like(acc_ref)

    def unpack(raw, out, i):
        part = WIDE

        def go(j, _):
            wide[0:part] = raw[i, pl.ds(pl.multiple_of(j * part, part), part), :].astype(f32)
            rows = pl.ds(pl.multiple_of(j * (part // 2), part // 2), part // 2)
            out[i, rows, 0:HD] = wide[pl.ds(0, part // 2, stride=2), :].astype(bf16)
            out[i, rows, HD:] = wide[pl.ds(1, part // 2, stride=2), :].astype(bf16)
            return 0

        lax.fori_loop(0, 2 * width // part, go, 0)

    def project(piece, x, owner, first):
        rows = pl.ds(piece * size, size)
        x = x.reshape(size, width)
        a = jnp.dot(x, wown[owner], preferred_element_type=f32)
        b = jnp.dot(x, wsib[owner], preferred_element_type=f32)
        if first:
            pown[rows, :] = a
            psib[rows, :] = b
        else:
            pown[rows, :] += a
            psib[rows, :] += b

    at_left = lax.rem(y + chips - 1, chips)
    at_right = lax.rem(y + 1, chips)
    at_far = lax.rem(y + 2, chips)
    forwards = []

    def forward(p):
        own_right[p].wait_recv()
        f = remote(
            hl.at[p, :, :, pl.ds(0, half)],
            ho.at[p, :, :, pl.ds(0, half)],
            fs_sem.at[p],
            frl_sem.at[p],
            (g, right),
        )
        f.start()
        forwards.append(f)
        if p + AHEAD < pieces:
            own_right[p + AHEAD].start()
        own_left[p].wait_recv()
        f = remote(
            hr.at[p, :, :, pl.ds(half, half)],
            ho.at[p, :, :, pl.ds(half, half)],
            fs_sem.at[pieces + p],
            frr_sem.at[p],
            (g, left),
        )
        f.start()
        forwards.append(f)
        if p + AHEAD < pieces:
            own_left[p + AHEAD].start()

    def near(p):
        project(p, hl[p], at_left, False)
        project(p, hr[p], at_right, False)

    exchange = []

    def far(p):
        for cols, sem in ((pl.ds(0, half), frl_sem), (pl.ds(half, half), frr_sem)):
            pltpu.make_async_copy(ho.at[p, :, :, cols], ho.at[p, :, :, cols], sem.at[p]).wait()
        project(p, ho[p], at_far, False)
        rows = pl.ds(p * size, size)
        x = remote(psib.at[rows], pget.at[rows], xs_sem.at[p], xr_sem.at[p], (g, sib))
        x.start()
        exchange.append(x)

    row = lax.broadcasted_iota(jnp.int32, (size, HD), 0)
    lane = lax.broadcasted_iota(jnp.int32, (size, HD), 1)
    block_of = row // STRIP
    start_of = jnp.where(block_of < blocks // 2, len0, len1) + (block_of & 1) * BLK + row % STRIP
    owners = [owner_ref[c, n] for n in (n0, n1) for c in range(2)]

    def choose(d):
        block = 0
        for e in range(1, len(owners)):
            block = jnp.where(owners[e] == d, e, block)
        return block

    def finish(p):
        rows = pl.ds(p * size, size)
        angle = (start_of + p * STRIP).astype(f32) * freq_ref[...]
        cosine = jnp.cos(angle)
        sine = jnp.where(lane < HD // 2, -1.0, 1.0) * jnp.sin(angle)
        exchange[p].wait_recv()
        kv = pown[rows, :] + pget[rows, :]
        k = kv[:, :HD]
        k = k * cosine + pltpu.roll(k, HD // 2, 1) * sine
        strip = pl.ds(p * STRIP, STRIP)
        nkv[:, 0, strip, :] = k.astype(bf16).reshape(blocks, STRIP, HD)
        nkv[:, 1, strip, :] = kv[:, HD:].astype(bf16).reshape(blocks, STRIP, HD)

    kept = []

    def push(p):
        strip = pl.ds(p * STRIP, STRIP)

        def go(k, _):
            d = lax.rem(g + k, groups)
            pbuf[p, d] = nkv[choose(d), :, p * STRIP : (p + 1) * STRIP, :]
            remote(
                pbuf.at[p, d], pushed_ref.at[g, :, strip], ps_sem.at[p], pr_sem.at[p], (d, t)
            ).start()
            return 0

        lax.fori_loop(1, groups, go, 0)
        pbuf[p, g] = nkv[choose(g), :, p * STRIP : (p + 1) * STRIP, :]
        keep = pltpu.make_async_copy(
            pbuf.at[p, g], pushed_ref.at[g, :, strip], loc_sem.at[4 + chips + p]
        )
        keep.start()
        kept.append(keep)

    def attend(rho, r):
        arr = arrs[rho]
        limit = (len0, len1)[r]

        def place(i, _):
            code = tab[groups + rho * PER_ROUND + i, r]
            block = code // groups
            holder = code % groups
            rows = pl.ds(pl.multiple_of(i * BLK, BLK), BLK)
            live = lax.broadcasted_iota(jnp.int32, (BLK, HD), 0) + block * BLK < limit
            kc[rows, 0:HD] = arr[holder, 0]
            kc[rows, HD : 2 * HD] = jnp.where(live, 0.0, MASKED).astype(bf16)
            vc[rows, 0:HD] = jnp.where(live, arr[holder, 1].astype(f32), 0.0).astype(bf16)
            vc[rows, HD : 2 * HD] = jnp.where(live, 1.0, 0.0).astype(bf16)
            return 0

        lax.fori_loop(0, PER_ROUND, place, 0)

        def score(h):
            q = qv[r * 2 * BLK : (r + 1) * 2 * BLK, h * HD : (h + 1) * HD]
            q = jnp.concatenate([q, jnp.ones_like(q)], axis=1)
            return lax.dot_general(
                q, kc[...], (((1,), (1,)), ((), ())), preferred_element_type=f32
            )

        ahead = score(0)
        for h in range(heads):
            scores = ahead
            if h + 1 < heads:
                ahead = score(h + 1)
            i = r * heads + h
            both = m_ref[i]
            old = jnp.broadcast_to(both[:, :1], both.shape)
            new = jnp.maximum(old, jnp.max(scores, axis=1, keepdims=True))
            alpha = jnp.exp2((old - new) * scale)
            w = jnp.exp2((scores - new[:, :1]) * scale).astype(bf16)
            o = jnp.dot(w, vc[...], preferred_element_type=f32)
            m_ref[i] = jnp.where(ml_lane, new, both * alpha + o[:, HD:])
            acc_ref[i] = acc_ref[i] * alpha + o[:, :HD]

    def arrived(rho):
        drain(arrs[rho].at[pl.ds(0, groups - 1)], ar_sem.at[rho])

    for c in local[3:]:
        c.wait()

    def own_weights(i, _):
        unpack(wraw_own, wown, i)
        return 0

    lax.fori_loop(0, chips, own_weights, 0)
    local[1].wait()
    local[2].wait()
    forward(0)
    for c in wcopies:
        c.wait()

    def swapped_weights(i, _):
        unpack(wraw_sib, wsib, i)
        return 0

    lax.fori_loop(0, chips, swapped_weights, 0)

    def own_piece(p, _):
        project(p, hown[:, pl.ds(pl.multiple_of(p * STRIP, STRIP), STRIP), :], y, True)
        return 0

    lax.fori_loop(0, pieces, own_piece, 0)

    forward(1)
    arrived(0)
    attend(0, 0)
    attend(0, 1)
    near(0)
    far(0)
    forward(2)
    arrived(1)
    attend(1, 0)
    finish(0)
    attend(1, 1)
    near(1)
    far(1)
    arrived(2)
    attend(2, 0)
    forward(3)
    finish(1)
    push(0)
    push(1)
    attend(2, 1)
    near(2)
    far(2)
    near(3)
    arrived(3)
    attend(3, 0)
    finish(2)
    push(2)
    far(3)
    finish(3)
    push(3)
    attend(3, 1)

    def fresh_request(r, _):
        kn = jnp.concatenate([nkv[2 * r, 0], nkv[2 * r + 1, 0]], axis=0)
        vn = jnp.concatenate([nkv[2 * r, 1], nkv[2 * r + 1, 1]], axis=0)
        vn = jnp.concatenate([vn, jnp.ones_like(vn)], axis=1)
        causal = lax.broadcasted_iota(jnp.int32, (2 * BLK, 2 * BLK), 1) <= (
            lax.broadcasted_iota(jnp.int32, (2 * BLK, 2 * BLK), 0)
        )

        def step(s, _):
            scores = []
            for u in range(HEADS_PER_STEP):
                h = s * HEADS_PER_STEP + u
                q = qv[
                    pl.ds(pl.multiple_of(r * 2 * BLK, 2 * BLK), 2 * BLK),
                    pl.ds(pl.multiple_of(h * HD, HD), HD),
                ]
                sc = lax.dot_general(
                    q, kn, (((1,), (1,)), ((), ())), preferred_element_type=f32
                )
                scores.append(jnp.where(causal, sc, MASKED))
            for u in range(HEADS_PER_STEP):
                h = s * HEADS_PER_STEP + u
                i = r * heads + h
                both = m_ref[i]
                old = jnp.broadcast_to(both[:, :1], both.shape)
                new = jnp.maximum(old, jnp.max(scores[u], axis=1, keepdims=True))
                alpha = jnp.exp2((old - new) * scale)
                w = jnp.exp2((scores[u] - new[:, :1]) * scale).astype(bf16)
                o = jnp.dot(w, vn, preferred_element_type=f32)
                total = jnp.broadcast_to(both[:, HD - 1 :], both.shape) * alpha + o[:, HD:]
                value = acc_ref[i] * alpha + o[:, :HD]
                att_ref[
                    pl.ds(pl.multiple_of(r * 2 * BLK, 2 * BLK), 2 * BLK),
                    pl.ds(pl.multiple_of(h * HD, HD), HD),
                ] = (value / total).astype(bf16)
            return 0

        lax.fori_loop(0, heads // HEADS_PER_STEP, step, 0)
        return 0

    lax.fori_loop(0, 2, fresh_request, 0)

    for p in range(pieces):
        own_right[p].wait_send()
        own_left[p].wait_send()
        exchange[p].wait_send()
    for f in forwards:
        f.wait_send()
    for rho in range(ROUNDS):
        drain(sbuf.at[rho, pl.ds(0, groups - 1)], as_sem.at[rho])
    for p in range(pieces):
        kept[p].wait()
        drain(pbuf.at[p, pl.ds(0, groups - 1)], ps_sem.at[p])
        drain(pushed_ref.at[pl.ds(0, groups - 1), :, pl.ds(p * STRIP, STRIP)], pr_sem.at[p])


def per_device(
    hidden,
    queries,
    keyval_weight,
    keyval_pool,
    prefix_len,
    slot_request,
    hit_holder,
    hit_slot,
    new_owner,
    new_slot,
):
    groups = lax.axis_size("grp")
    rows, width = hidden.shape
    chips = lax.axis_size("tp") // 2
    blocks = rows // BLK
    pieces = BLK // STRIP
    hidden = hidden.reshape(blocks, BLK, width)
    heads = queries.shape[1] // HD
    pool_slots = keyval_pool.shape[0]
    pool = keyval_pool.reshape(pool_slots, 2, BLK, HD)
    weight = keyval_weight.reshape(-1, HD)

    frequency = ROPE_BASE ** (-(np.arange(HD // 2) * 2.0 / HD))
    frequency = jnp.asarray(np.concatenate([frequency, frequency])[None, :], f32)

    smem = pl.BlockSpec(memory_space=pltpu.SMEM)
    vmem = pl.BlockSpec(memory_space=pltpu.VMEM)
    anym = pl.BlockSpec(memory_space=pl.ANY)
    dma = pltpu.SemaphoreType.DMA
    V = pltpu.VMEM

    attention, pushed = pl.pallas_call(
        main_kernel,
        out_shape=(
            jax.ShapeDtypeStruct(queries.shape, bf16),
            jax.ShapeDtypeStruct((groups, 2, BLK, HD), bf16),
        ),
        in_specs=[smem, smem, smem, vmem, vmem, vmem, anym, anym, anym, anym],
        out_specs=(vmem, anym),
        scratch_shapes=[V((groups, 2, BLK, HD), bf16)] * ROUNDS
        + [
            V(pool.shape, bf16),
            V((ROUNDS, groups, 2, BLK, HD), bf16),
            V((4, groups, HD), jnp.int32),
            V((groups + MAXB, HD), jnp.int32),
            pltpu.SMEM((groups + MAXB, HD), jnp.int32),
            V(queries.shape, bf16),
            V((blocks, BLK, width), bf16),
            V((pieces, blocks, STRIP, width), bf16),
            V((pieces, blocks, STRIP, width), bf16),
            V((pieces, blocks, STRIP, width), bf16),
            V((chips, 2 * width, HD), bf16),
            V((chips, 2 * width, HD), bf16),
            V((WIDE + 8, HD), f32),
            V((chips, width, 2 * HD), bf16),
            V((chips, width, 2 * HD), bf16),
            V((rows, 2 * HD), f32),
            V((rows, 2 * HD), f32),
            V((rows, 2 * HD), f32),
            V((PER_ROUND * BLK, 2 * HD), bf16),
            V((PER_ROUND * BLK, 2 * HD), bf16),
            V((2 * heads, 2 * BLK, HD), f32),
            V((2 * heads, 2 * BLK, HD), f32),
            V((blocks, 2, BLK, HD), bf16),
            V((pieces, groups, 2, STRIP, HD), bf16),
            dma((4 + chips + pieces,)),
            dma((chips,)),
            dma((chips,)),
            dma((pieces,)),
            dma((pieces,)),
            dma((pieces,)),
            dma((pieces,)),
            dma((2 * pieces,)),
            dma((pieces,)),
            dma((pieces,)),
            dma((ROUNDS,)),
            dma((ROUNDS,)),
            dma((pieces,)),
            dma((pieces,)),
            dma((pieces,)),
            dma((pieces,)),
        ],
        compiler_params=pltpu.CompilerParams(
            collective_id=0, has_side_effects=True, vmem_limit_bytes=62 * 2**20
        ),
    )(
        slot_request,
        prefix_len,
        new_owner.T,
        frequency,
        hit_holder,
        hit_slot,
        hidden,
        queries,
        weight,
        pool,
    )

    parts = 20
    new_pool = pl.pallas_call(
        store_kernel,
        out_shape=jax.ShapeDtypeStruct(pool.shape, bf16),
        in_specs=[smem, smem, smem, anym, anym],
        out_specs=anym,
        scratch_shapes=[
            V(pool.shape, bf16),
            V((groups, 2, BLK, HD), bf16),
            dma((parts,)),
            dma((parts,)),
            dma,
        ],
        compiler_params=pltpu.CompilerParams(vmem_limit_bytes=62 * 2**20),
    )(slot_request, new_owner.T, new_slot.T, pool, pushed)
    return attention, new_pool.reshape(keyval_pool.shape)


def solution(mesh):
    in_specs = (
        P("grp", "tp"),
        P("grp", "tp"),
        P(None, None, "tp"),
        P("grp", None, "tp", None, None),
        P(),
        P(),
        P(),
        P(),
        P(),
        P(),
    )
    out_specs = (P("grp", "tp"), P("grp", None, "tp", None, None))
    return jax.shard_map(
        per_device, mesh=mesh, in_specs=in_specs, out_specs=out_specs, check_vma=False
    )
```

```python
import functools
import math

import jax
import jax.numpy as jnp
import numpy as np
from jax import lax
from jax.experimental import pallas as pl
from jax.experimental.pallas import tpu as pltpu
from jax.sharding import PartitionSpec as P

MESH = pl.DeviceIdType.MESH
ROPE_BASE = 1000000.0
MASKED = -1e30
BLK = 128
HD = 128
ROUNDS = 4
PER_ROUND = 8
HEADS_PER_STEP = 6
MAXB = 32
WIDE = 512
STRIP = 32
AHEAD = 2
bf16 = jnp.bfloat16
f32 = jnp.float32


def remote(src, dst, send_sem, recv_sem, device):
    return pltpu.make_async_remote_copy(
        src_ref=src,
        dst_ref=dst,
        send_sem=send_sem,
        recv_sem=recv_sem,
        device_id=device,
        device_id_type=MESH,
    )


def drain(ref, sem):
    pltpu.make_async_copy(ref, ref, sem).wait()


def store_kernel(
    request_ref, owner_ref, slot_ref, pool_ref, pushed_ref, out_ref, pool, pushed, in_sem, out_sem, push_sem
):
    count = pushed_ref.shape[0]
    limit = out_ref.shape[0]
    parts = in_sem.shape[0]
    size = limit // parts
    me = lax.axis_index("grp")
    loads = [
        pltpu.make_async_copy(
            pool_ref.at[pl.ds(i * size, size)], pool.at[pl.ds(i * size, size)], in_sem.at[i]
        )
        for i in range(parts)
    ]
    stores = [
        pltpu.make_async_copy(
            pool.at[pl.ds(i * size, size)], out_ref.at[pl.ds(i * size, size)], out_sem.at[i]
        )
        for i in range(parts)
    ]
    fetch = pltpu.make_async_copy(pushed_ref, pushed, push_sem)
    for c in loads:
        c.start()
    fetch.start()

    def target(i):
        row = limit
        for r in range(2):
            n = request_ref[2 * i + r]
            for c in range(2):
                row = jnp.where(owner_ref[c, n] == me, slot_ref[c, n], row)
        return row

    for c in loads:
        c.wait()
    fetch.wait()

    def patch(i, _):
        row = target(i)

        @pl.when(row < limit)
        def _():
            pool[row] = pushed[i]

        return 0

    lax.fori_loop(0, count, patch, 0)
    for c in stores:
        c.start()
    for c in stores:
        c.wait()


def running_count(marks):
    lane = lax.broadcasted_iota(jnp.int32, marks.shape, 1)
    total = marks
    for shift in (1, 2, 4, 8, 16):
        total = total + jnp.where(lane >= shift, pltpu.roll(total, shift, 1), 0)
    return total - marks


def rows_to_send(h0, h1, s0, s1, me):
    e0 = (h0 == me).astype(jnp.int32)
    e1 = (h1 == me).astype(jnp.int32)
    start = jnp.sum(((h0 >= 0) & (h0 < me)).astype(jnp.int32), axis=1, keepdims=True)
    mine = jnp.sum(e0, axis=1, keepdims=True)
    turn0 = (running_count(e0) + start) & (ROUNDS - 1)
    turn1 = (running_count(e1) + (start + mine)) & (ROUNDS - 1)
    lane = lax.broadcasted_iota(jnp.int32, h0.shape, 1)
    rows = jnp.zeros_like(h0)
    for rho in range(ROUNDS):
        chosen = jnp.where((e0 == 1) & (turn0 == rho), s0, 0) + jnp.where(
            (e1 == 1) & (turn1 == rho), s1, 0
        )
        rows = jnp.where(lane == rho, jnp.sum(chosen, axis=1, keepdims=True), rows)
    return rows


def blocks_to_read(h0, h1, groups):
    count = MAXB
    sub = lax.broadcasted_iota(jnp.int32, (count, HD), 0)
    lane = lax.broadcasted_iota(jnp.int32, (count, HD), 1)
    inside = lane < count
    eye = sub == lane
    h0 = jnp.broadcast_to(h0, (count, HD))
    h1 = jnp.broadcast_to(h1, (count, HD))
    h0_col = jnp.sum(jnp.where(eye, h0, 0), axis=1, keepdims=True)
    h1_col = jnp.sum(jnp.where(eye, h1, 0), axis=1, keepdims=True)

    def over_rows(mark):
        return jnp.sum(mark.astype(jnp.int32), axis=0, keepdims=True)

    rank0 = over_rows((h0_col == h0) & (sub < lane))
    rank1 = over_rows((h1_col == h1) & (sub < lane))
    below0 = over_rows(h0_col < h0)
    below1 = over_rows(h0_col < h1)
    upto1 = over_rows(h0_col <= h1)
    index0 = below0 + rank0
    place0 = (index0 & (ROUNDS - 1)) * PER_ROUND + (index0 >> 2)
    turn1 = (upto1 + rank1) & (ROUNDS - 1)
    place1 = turn1 * PER_ROUND + h1[0:1] - ((below1 + (ROUNDS - 1) - turn1) >> 2)
    code0 = lane * groups + h0
    code1 = lane * groups + h1
    col0 = jnp.sum(jnp.where((place0 == sub) & inside, code0, 0), axis=1, keepdims=True)
    col1 = jnp.sum(jnp.where((place1 == sub) & inside, code1, 0), axis=1, keepdims=True)
    return jnp.where(lane == 0, col0, jnp.where(lane == 1, col1, 0))


def main_kernel(
    request_ref,
    length_ref,
    owner_ref,
    freq_ref,
    holder_ref,
    slot_ref,
    hid_ref,
    q_hbm,
    w_ref,
    pool_ref,
    att_ref,
    pushed_ref,
    arr0,
    arr1,
    arr2,
    arr3,
    pool,
    sbuf,
    hs,
    tab_v,
    tab,
    qv,
    hown,
    hl,
    hr,
    ho,
    wraw_own,
    wraw_sib,
    wide,
    wown,
    wsib,
    pown,
    psib,
    pget,
    kc,
    vc,
    m_ref,
    acc_ref,
    nkv,
    pbuf,
    loc_sem,
    ws_sem,
    wr_sem,
    ls_sem,
    lr_sem,
    rs_sem,
    rr_sem,
    fs_sem,
    frl_sem,
    frr_sem,
    as_sem,
    ar_sem,
    xs_sem,
    xr_sem,
    ps_sem,
    pr_sem,
):
    groups = lax.axis_size("grp")
    arrs = (arr0, arr1, arr2, arr3)
    g = lax.axis_index("grp")
    t = lax.axis_index("tp")
    chips = lax.axis_size("tp") // 2
    y = t // 2
    core = t % 2
    right = lax.rem(y + 1, chips) * 2 + core
    left = lax.rem(y + chips - 1, chips) * 2 + core
    sib = y * 2 + 1 - core
    blocks, _, width = hid_ref.shape
    half = width // 2
    pieces = BLK // STRIP
    size = blocks * STRIP
    heads = q_hbm.shape[1] // HD
    scale = math.log2(math.e) / math.sqrt(HD)

    local = [
        pltpu.make_async_copy(pool_ref, pool, loc_sem.at[0]),
        pltpu.make_async_copy(hid_ref, hown, loc_sem.at[1]),
        pltpu.make_async_copy(q_hbm, qv, loc_sem.at[2]),
    ]
    for i in range(chips):
        local.append(
            pltpu.make_async_copy(
                w_ref.at[pl.ds((2 * i + core) * (2 * width), 2 * width)],
                wraw_own.at[i],
                loc_sem.at[3 + i],
            )
        )
    local[0].start()

    barrier = pltpu.get_barrier_semaphore()

    def greet(k, _):
        pl.semaphore_signal(
            barrier, inc=1, device_id=(lax.rem(g + k, groups), t), device_id_type=MESH
        )
        return 0

    lax.fori_loop(1, groups, greet, 0)
    for peer in (right, left, sib):
        pl.semaphore_signal(barrier, inc=1, device_id=(g, peer), device_id_type=MESH)
    hs[...] = jnp.full_like(hs, -1)

    def in_order(i, _):
        for r in range(2):
            n = request_ref[2 * i + r]
            hs[r, pl.ds(i, 1), 0:MAXB] = holder_ref[pl.ds(n, 1), :]
            hs[2 + r, pl.ds(i, 1), 0:MAXB] = slot_ref[pl.ds(n, 1), :]
        return 0

    lax.fori_loop(0, groups, in_order, 0)
    tab_v[0:groups] = rows_to_send(hs[0], hs[1], hs[2], hs[3], g)
    tab_v[groups:] = blocks_to_read(hs[0, pl.ds(g, 1), :], hs[1, pl.ds(g, 1), :], groups)
    to_smem = pltpu.make_async_copy(tab_v, tab, loc_sem.at[3 + chips])
    to_smem.start()
    pl.semaphore_wait(barrier, groups + 2)

    own_right = []
    own_left = []
    for p in range(pieces):
        strip = hid_ref.at[:, pl.ds(p * STRIP, STRIP)]
        own_right.append(remote(strip, hl.at[p], ls_sem.at[p], lr_sem.at[p], (g, right)))
        own_left.append(remote(strip, hr.at[p], rs_sem.at[p], rr_sem.at[p], (g, left)))
    for p in range(AHEAD):
        own_right[p].start()
        own_left[p].start()

    to_smem.wait()
    n0 = request_ref[2 * g]
    n1 = request_ref[2 * g + 1]
    len0 = length_ref[n0]
    len1 = length_ref[n1]

    local[0].wait()
    for rho in range(ROUNDS):
        arr = arrs[rho]

        def fill(k, _, rho=rho, arr=arr):
            d = lax.rem(g + k, groups)
            sbuf[rho, d] = pool[tab[d, rho]]
            remote(sbuf.at[rho, d], arr.at[g], as_sem.at[rho], ar_sem.at[rho], (d, t)).start()
            return 0

        lax.fori_loop(1, groups, fill, 0)
        arr[g] = pool[tab[g, rho]]

    wcopies = []
    for i in range(chips):
        wcopies.append(
            remote(
                w_ref.at[pl.ds((2 * i + 1 - core) * (2 * width), 2 * width)],
                wraw_sib.at[i],
                ws_sem.at[i],
                wr_sem.at[i],
                (g, sib),
            )
        )
        wcopies[-1].start()

    for c in local[1:]:
        c.start()
    m_ref[...] = jnp.full_like(m_ref, MASKED)
    acc_ref[...] = jnp.zeros_like(acc_ref)

    def unpack(raw, out, i):
        part = WIDE

        def go(j, _):
            wide[0:part] = raw[i, pl.ds(pl.multiple_of(j * part, part), part), :].astype(f32)
            rows = pl.ds(pl.multiple_of(j * (part // 2), part // 2), part // 2)
            out[i, rows, 0:HD] = wide[pl.ds(0, part // 2, stride=2), :].astype(bf16)
            out[i, rows, HD:] = wide[pl.ds(1, part // 2, stride=2), :].astype(bf16)
            return 0

        lax.fori_loop(0, 2 * width // part, go, 0)

    def project(piece, x, owner, first):
        rows = pl.ds(piece * size, size)
        x = x.reshape(size, width)
        a = jnp.dot(x, wown[owner], preferred_element_type=f32)
        b = jnp.dot(x, wsib[owner], preferred_element_type=f32)
        if first:
            pown[rows, :] = a
            psib[rows, :] = b
        else:
            pown[rows, :] += a
            psib[rows, :] += b

    at_left = lax.rem(y + chips - 1, chips)
    at_right = lax.rem(y + 1, chips)
    at_far = lax.rem(y + 2, chips)
    forwards = []

    def forward(p):
        own_right[p].wait_recv()
        f = remote(
            hl.at[p, :, :, pl.ds(0, half)],
            ho.at[p, :, :, pl.ds(0, half)],
            fs_sem.at[p],
            frl_sem.at[p],
            (g, right),
        )
        f.start()
        forwards.append(f)
        if p + AHEAD < pieces:
            own_right[p + AHEAD].start()
        own_left[p].wait_recv()
        f = remote(
            hr.at[p, :, :, pl.ds(half, half)],
            ho.at[p, :, :, pl.ds(half, half)],
            fs_sem.at[pieces + p],
            frr_sem.at[p],
            (g, left),
        )
        f.start()
        forwards.append(f)
        if p + AHEAD < pieces:
            own_left[p + AHEAD].start()

    def near(p):
        project(p, hl[p], at_left, False)
        project(p, hr[p], at_right, False)

    exchange = []

    def far(p):
        for cols, sem in ((pl.ds(0, half), frl_sem), (pl.ds(half, half), frr_sem)):
            pltpu.make_async_copy(ho.at[p, :, :, cols], ho.at[p, :, :, cols], sem.at[p]).wait()
        project(p, ho[p], at_far, False)
        rows = pl.ds(p * size, size)
        x = remote(psib.at[rows], pget.at[rows], xs_sem.at[p], xr_sem.at[p], (g, sib))
        x.start()
        exchange.append(x)

    row = lax.broadcasted_iota(jnp.int32, (size, HD), 0)
    lane = lax.broadcasted_iota(jnp.int32, (size, HD), 1)
    block_of = row // STRIP
    start_of = jnp.where(block_of < blocks // 2, len0, len1) + (block_of & 1) * BLK + row % STRIP
    owners = [owner_ref[c, n] for n in (n0, n1) for c in range(2)]

    def choose(d):
        block = 0
        for e in range(1, len(owners)):
            block = jnp.where(owners[e] == d, e, block)
        return block

    def finish(p):
        rows = pl.ds(p * size, size)
        angle = (start_of + p * STRIP).astype(f32) * freq_ref[...]
        cosine = jnp.cos(angle)
        sine = jnp.where(lane < HD // 2, -1.0, 1.0) * jnp.sin(angle)
        exchange[p].wait_recv()
        kv = pown[rows, :] + pget[rows, :]
        k = kv[:, :HD]
        k = k * cosine + pltpu.roll(k, HD // 2, 1) * sine
        strip = pl.ds(p * STRIP, STRIP)
        nkv[:, 0, strip, :] = k.astype(bf16).reshape(blocks, STRIP, HD)
        nkv[:, 1, strip, :] = kv[:, HD:].astype(bf16).reshape(blocks, STRIP, HD)

    kept = []

    def push(p):
        strip = pl.ds(p * STRIP, STRIP)

        def go(k, _):
            d = lax.rem(g + k, groups)
            pbuf[p, d] = nkv[choose(d), :, p * STRIP : (p + 1) * STRIP, :]
            remote(
                pbuf.at[p, d], pushed_ref.at[g, :, strip], ps_sem.at[p], pr_sem.at[p], (d, t)
            ).start()
            return 0

        lax.fori_loop(1, groups, go, 0)
        pbuf[p, g] = nkv[choose(g), :, p * STRIP : (p + 1) * STRIP, :]
        keep = pltpu.make_async_copy(
            pbuf.at[p, g], pushed_ref.at[g, :, strip], loc_sem.at[4 + chips + p]
        )
        keep.start()
        kept.append(keep)

    def attend(rho, r):
        arr = arrs[rho]
        limit = (len0, len1)[r]

        def place(i, _):
            code = tab[groups + rho * PER_ROUND + i, r]
            block = code // groups
            holder = code % groups
            rows = pl.ds(pl.multiple_of(i * BLK, BLK), BLK)
            live = lax.broadcasted_iota(jnp.int32, (BLK, HD), 0) + block * BLK < limit
            kc[rows, 0:HD] = arr[holder, 0]
            kc[rows, HD : 2 * HD] = jnp.where(live, 0.0, MASKED).astype(bf16)
            vc[rows, 0:HD] = jnp.where(live, arr[holder, 1].astype(f32), 0.0).astype(bf16)
            vc[rows, HD : 2 * HD] = jnp.where(live, 1.0, 0.0).astype(bf16)
            return 0

        lax.fori_loop(0, PER_ROUND, place, 0)

        def step(s, _):
            scores = []
            for u in range(HEADS_PER_STEP):
                h = s * HEADS_PER_STEP + u
                q = qv[r * 2 * BLK : (r + 1) * 2 * BLK, pl.ds(pl.multiple_of(h * HD, HD), HD)]
                q = jnp.concatenate([q, jnp.ones_like(q)], axis=1)
                scores.append(
                    lax.dot_general(
                        q, kc[...], (((1,), (1,)), ((), ())), preferred_element_type=f32
                    )
                )
            for u in range(HEADS_PER_STEP):
                i = r * heads + s * HEADS_PER_STEP + u
                old = m_ref[i]
                new = jnp.maximum(old, jnp.max(scores[u], axis=1, keepdims=True))
                alpha = jnp.exp2((old - new) * scale)
                w = jnp.exp2((scores[u] - new[:, :1]) * scale).astype(bf16)
                o = jnp.dot(w, vc[...], preferred_element_type=f32)
                m_ref[i] = new
                acc_ref[i, :, 0:HD] = acc_ref[i, :, 0:HD] * alpha + o[:, :HD]
                acc_ref[i, :, HD:] = acc_ref[i, :, HD:] * alpha + o[:, HD:]
            return 0

        lax.fori_loop(0, heads // HEADS_PER_STEP, step, 0)

    def arrived(rho):
        drain(arrs[rho].at[pl.ds(0, groups - 1)], ar_sem.at[rho])

    for c in local[3:]:
        c.wait()

    def own_weights(i, _):
        unpack(wraw_own, wown, i)
        return 0

    lax.fori_loop(0, chips, own_weights, 0)
    local[1].wait()
    local[2].wait()
    forward(0)
    for c in wcopies:
        c.wait()

    def swapped_weights(i, _):
        unpack(wraw_sib, wsib, i)
        return 0

    lax.fori_loop(0, chips, swapped_weights, 0)

    def own_piece(p, _):
        project(p, hown[:, pl.ds(pl.multiple_of(p * STRIP, STRIP), STRIP), :], y, True)
        return 0

    lax.fori_loop(0, pieces, own_piece, 0)

    forward(1)
    arrived(0)
    attend(0, 0)
    attend(0, 1)
    near(0)
    far(0)
    forward(2)
    arrived(1)
    attend(1, 0)
    finish(0)
    attend(1, 1)
    near(1)
    far(1)
    arrived(2)
    attend(2, 0)
    forward(3)
    finish(1)
    push(0)
    push(1)
    attend(2, 1)
    near(2)
    far(2)
    near(3)
    arrived(3)
    attend(3, 0)
    finish(2)
    push(2)
    far(3)
    finish(3)
    push(3)
    attend(3, 1)

    def fresh_request(r, _):
        kn = jnp.concatenate([nkv[2 * r, 0], nkv[2 * r + 1, 0]], axis=0)
        vn = jnp.concatenate([nkv[2 * r, 1], nkv[2 * r + 1, 1]], axis=0)
        vn = jnp.concatenate([vn, jnp.ones_like(vn)], axis=1)
        causal = lax.broadcasted_iota(jnp.int32, (2 * BLK, 2 * BLK), 1) <= (
            lax.broadcasted_iota(jnp.int32, (2 * BLK, 2 * BLK), 0)
        )

        def step(s, _):
            scores = []
            for u in range(HEADS_PER_STEP):
                h = s * HEADS_PER_STEP + u
                q = qv[
                    pl.ds(pl.multiple_of(r * 2 * BLK, 2 * BLK), 2 * BLK),
                    pl.ds(pl.multiple_of(h * HD, HD), HD),
                ]
                sc = lax.dot_general(
                    q, kn, (((1,), (1,)), ((), ())), preferred_element_type=f32
                )
                scores.append(jnp.where(causal, sc, MASKED))
            for u in range(HEADS_PER_STEP):
                h = s * HEADS_PER_STEP + u
                i = r * heads + h
                old = m_ref[i]
                new = jnp.maximum(old, jnp.max(scores[u], axis=1, keepdims=True))
                alpha = jnp.exp2((old - new) * scale)
                w = jnp.exp2((scores[u] - new[:, :1]) * scale).astype(bf16)
                o = jnp.dot(w, vn, preferred_element_type=f32)
                total = acc_ref[i, :, HD:] * alpha + o[:, HD:]
                value = acc_ref[i, :, 0:HD] * alpha + o[:, :HD]
                att_ref[
                    pl.ds(pl.multiple_of(r * 2 * BLK, 2 * BLK), 2 * BLK),
                    pl.ds(pl.multiple_of(h * HD, HD), HD),
                ] = (value / total).astype(bf16)
            return 0

        lax.fori_loop(0, heads // HEADS_PER_STEP, step, 0)
        return 0

    lax.fori_loop(0, 2, fresh_request, 0)

    for p in range(pieces):
        own_right[p].wait_send()
        own_left[p].wait_send()
        exchange[p].wait_send()
    for f in forwards:
        f.wait_send()
    for rho in range(ROUNDS):
        drain(sbuf.at[rho, pl.ds(0, groups - 1)], as_sem.at[rho])
    for p in range(pieces):
        kept[p].wait()
        drain(pbuf.at[p, pl.ds(0, groups - 1)], ps_sem.at[p])
        drain(pushed_ref.at[pl.ds(0, groups - 1), :, pl.ds(p * STRIP, STRIP)], pr_sem.at[p])


def per_device(
    hidden,
    queries,
    keyval_weight,
    keyval_pool,
    prefix_len,
    slot_request,
    hit_holder,
    hit_slot,
    new_owner,
    new_slot,
):
    groups = lax.axis_size("grp")
    rows, width = hidden.shape
    chips = lax.axis_size("tp") // 2
    blocks = rows // BLK
    pieces = BLK // STRIP
    hidden = hidden.reshape(blocks, BLK, width)
    heads = queries.shape[1] // HD
    pool_slots = keyval_pool.shape[0]
    pool = keyval_pool.reshape(pool_slots, 2, BLK, HD)
    weight = keyval_weight.reshape(-1, HD)

    frequency = ROPE_BASE ** (-(np.arange(HD // 2) * 2.0 / HD))
    frequency = jnp.asarray(np.concatenate([frequency, frequency])[None, :], f32)

    smem = pl.BlockSpec(memory_space=pltpu.SMEM)
    vmem = pl.BlockSpec(memory_space=pltpu.VMEM)
    anym = pl.BlockSpec(memory_space=pl.ANY)
    dma = pltpu.SemaphoreType.DMA
    V = pltpu.VMEM

    attention, pushed = pl.pallas_call(
        main_kernel,
        out_shape=(
            jax.ShapeDtypeStruct(queries.shape, bf16),
            jax.ShapeDtypeStruct((groups, 2, BLK, HD), bf16),
        ),
        in_specs=[smem, smem, smem, vmem, vmem, vmem, anym, anym, anym, anym],
        out_specs=(vmem, anym),
        scratch_shapes=[V((groups, 2, BLK, HD), bf16)] * ROUNDS
        + [
            V(pool.shape, bf16),
            V((ROUNDS, groups, 2, BLK, HD), bf16),
            V((4, groups, HD), jnp.int32),
            V((groups + MAXB, HD), jnp.int32),
            pltpu.SMEM((groups + MAXB, HD), jnp.int32),
            V(queries.shape, bf16),
            V((blocks, BLK, width), bf16),
            V((pieces, blocks, STRIP, width), bf16),
            V((pieces, blocks, STRIP, width), bf16),
            V((pieces, blocks, STRIP, width), bf16),
            V((chips, 2 * width, HD), bf16),
            V((chips, 2 * width, HD), bf16),
            V((WIDE + 8, HD), f32),
            V((chips, width, 2 * HD), bf16),
            V((chips, width, 2 * HD), bf16),
            V((rows, 2 * HD), f32),
            V((rows, 2 * HD), f32),
            V((rows, 2 * HD), f32),
            V((PER_ROUND * BLK, 2 * HD), bf16),
            V((PER_ROUND * BLK, 2 * HD), bf16),
            V((2 * heads, 2 * BLK, HD), f32),
            V((2 * heads, 2 * BLK, 2 * HD), f32),
            V((blocks, 2, BLK, HD), bf16),
            V((pieces, groups, 2, STRIP, HD), bf16),
            dma((4 + chips + pieces,)),
            dma((chips,)),
            dma((chips,)),
            dma((pieces,)),
            dma((pieces,)),
            dma((pieces,)),
            dma((pieces,)),
            dma((2 * pieces,)),
            dma((pieces,)),
            dma((pieces,)),
            dma((ROUNDS,)),
            dma((ROUNDS,)),
            dma((pieces,)),
            dma((pieces,)),
            dma((pieces,)),
            dma((pieces,)),
        ],
        compiler_params=pltpu.CompilerParams(
            collective_id=0, has_side_effects=True, vmem_limit_bytes=62 * 2**20
        ),
    )(
        slot_request,
        prefix_len,
        new_owner.T,
        frequency,
        hit_holder,
        hit_slot,
        hidden,
        queries,
        weight,
        pool,
    )

    parts = 20
    new_pool = pl.pallas_call(
        store_kernel,
        out_shape=jax.ShapeDtypeStruct(pool.shape, bf16),
        in_specs=[smem, smem, smem, anym, anym],
        out_specs=anym,
        scratch_shapes=[
            V(pool.shape, bf16),
            V((groups, 2, BLK, HD), bf16),
            dma((parts,)),
            dma((parts,)),
            dma,
        ],
        compiler_params=pltpu.CompilerParams(vmem_limit_bytes=62 * 2**20),
    )(slot_request, new_owner.T, new_slot.T, pool, pushed)
    return attention, new_pool.reshape(keyval_pool.shape)


def solution(mesh):
    in_specs = (
        P("grp", "tp"),
        P("grp", "tp"),
        P(None, None, "tp"),
        P("grp", None, "tp", None, None),
        P(),
        P(),
        P(),
        P(),
        P(),
        P(),
    )
    out_specs = (P("grp", "tp"), P("grp", None, "tp", None, None))
    return jax.shard_map(
        per_device, mesh=mesh, in_specs=in_specs, out_specs=out_specs, check_vma=False
    )
```
